128 devices in a mesh: grp: 8 (over y, core), blk: 16 (over x, z).
Axes of the slice: x: 4, y: 4, z: 4, core: 2. Of those that a mesh axis runs over, the one named last changes fastest.
Arguments:
- embeddings: float32 [65536, 1024], P(('grp', 'blk'))
- cluster_id: int32 [65536], P(('grp', 'blk')), may hold values from 0 to 63, as said below
- cluster_group: int32 [64], replicated, may hold values from 0 to 7, as said below
Outputs:
- max_cos: float32 [65536], P(('grp', 'blk'))
- log_mass: float32 [65536], P(('grp', 'blk'))
The draws below stay inside these ranges and needn't reach their ends.
Inputs may be any that keep to these rules, and one draw needn't show every extreme that they name: `cluster_id`: among the rows of one device, at most 96 name clusters that cluster_group maps to one group; for some group exactly 96. `cluster_group`: each group owns 8 clusters.
All inputs are finite; a program needn't handle non-finite values.
Results may differ from the reference program's by a relative error of at most 0.00042.
Values may be sent and summed in bfloat16 or wider, within the bound.
A program may use at most 128 MiB of HBM per device.

```python
import jax
import jax.numpy as jnp
from jax import lax

D = 1024
CL_GRP = 8
ROW_DEV = 512
CLUSTERS = 64
CAP = 96
ROWS = 65536
N_GRP = 8
DEVICES = 128


def shared_order(key):
    return jax.random.permutation(key, CLUSTERS).astype(jnp.int32)


def one_block(key, order):
    keys = jax.random.split(key, 5)
    first = jax.random.randint(keys[0], (), 0, N_GRP)
    others = jax.random.permutation(keys[1], (N_GRP - 1) * CAP)[:ROW_DEV - CAP] // CAP
    others = others + (others >= first).astype(jnp.int32)
    groups = jnp.concatenate([jnp.full((CAP,), first, jnp.int32), others.astype(jnp.int32)])
    groups = jax.random.permutation(keys[2], groups)
    left = jax.random.randint(keys[3], (ROW_DEV,), 0, CL_GRP)
    right = jax.random.randint(keys[4], (ROW_DEV,), 0, CL_GRP)
    within = left * right // CL_GRP
    return order[groups * CL_GRP + within]


def cluster_rows(key):
    order = shared_order(key)
    sub = jax.random.fold_in(key, 7)
    keys = jax.random.split(sub, DEVICES)
    blocks = jax.vmap(lambda k: one_block(k, order))(keys)
    return blocks.reshape(-1).astype(jnp.int32)


def draw_cluster_group(key, part):
    order = shared_order(key)
    inverse = jnp.zeros((CLUSTERS,), jnp.int32).at[order].set(jnp.arange(CLUSTERS, dtype=jnp.int32))
    return (inverse // CL_GRP).astype(jnp.int32)


def draw_cluster_id(key, part):
    labels = cluster_rows(key)
    return labels


def draw_embeddings(key, part):
    labels = cluster_rows(key)
    key = jax.random.fold_in(key, 11)
    keys = jax.random.split(key, 6)
    noise = jax.random.truncated_normal(keys[0], -6.0, 6.0, (ROWS, D), jnp.float32)
    base = noise
    positions = jnp.arange(ROWS, dtype=jnp.int32)
    order = jnp.argsort(labels, stable=True).astype(jnp.int32)
    previous = jnp.concatenate([order[:1], order[:-1]])
    partner = jnp.zeros((ROWS,), jnp.int32).at[order].set(previous)
    same = labels[partner] == labels
    chosen = (jax.random.randint(keys[3], (ROWS,), 0, 16) == 0) & same & (partner != positions)
    spread = jax.random.uniform(keys[4], (ROWS, 1), jnp.float32, 0.15, 0.6)
    extra = jax.random.truncated_normal(keys[5], -6.0, 6.0, (ROWS, D), jnp.float32)
    copies = base[partner] + spread * extra
    return jnp.where(chosen[:, None], copies, base).astype(jnp.float32)


def setup_inputs(seed: int = 0) -> dict:
    key_of = jax.random.split(jax.random.key(seed), 4)
    embeddings = draw_embeddings(jax.random.fold_in(key_of[3], 71), 0)
    cluster_id = draw_cluster_id(jax.random.fold_in(key_of[3], 71), 0)
    cluster_group = draw_cluster_group(jax.random.fold_in(key_of[3], 71), 0)
    return {"embeddings": embeddings, "cluster_id": cluster_id, "cluster_group": cluster_group}


def reference(embeddings, cluster_id, cluster_group):
    rows = embeddings.shape[0]
    unit = (embeddings * lax.rsqrt(lax.optimization_barrier(jnp.sum(embeddings * embeddings, axis=1, keepdims=True)) + 1e-06)).astype(jnp.bfloat16)
    target = cluster_group[cluster_id].astype(jnp.int32)
    keys = target * rows + jnp.arange(rows, dtype=jnp.int32)
    order = jnp.argsort(keys, stable=True).astype(jnp.int32)
    counts = lax.optimization_barrier(jnp.sum((target[:, None] == jnp.arange(N_GRP, dtype=jnp.int32)[None, :]).astype(jnp.int32), axis=0))
    starts = jnp.cumsum(counts) - counts
    span = DEVICES * CAP
    block = min(512, span)

    def per_group(group):
        places = jnp.arange(span, dtype=jnp.int32)
        live = places < counts[group]
        where_at = jnp.minimum(starts[group] + places, rows - 1).astype(jnp.int32)
        index = jnp.where(live, order[where_at], rows).astype(jnp.int32)
        safe = jnp.minimum(index, rows - 1)
        units_g = unit[safe]
        tags_g = jnp.where(live, cluster_id[safe], -1)

        def per_block(number):
            low = (number * block).astype(jnp.int32)
            left = lax.dynamic_slice_in_dim(units_g, low, block, 0)
            left_tags = lax.dynamic_slice_in_dim(tags_g, low, block, 0)
            scores = jnp.dot(left, units_g.T, preferred_element_type=jnp.float32)
            same = (left_tags[:, None] == tags_g[None, :]) & (left_tags[:, None] >= 0)
            selfs = (low + jnp.arange(block, dtype=jnp.int32))[:, None] == places[None, :]
            other = same & jnp.logical_not(selfs)
            best = lax.optimization_barrier(jnp.max(jnp.where(other, scores, jnp.float32(-1.0)), axis=1))
            total = lax.optimization_barrier(jnp.sum(jnp.where(other, jnp.exp(20.0 * scores), jnp.float32(0.0)), axis=1))
            return (best, jnp.log(1.0 + total))
        best, mass = lax.map(per_block, jnp.arange(span // block, dtype=jnp.int32))
        return (best.reshape(-1), mass.reshape(-1), index)
    bests, masses, indexes = lax.map(per_group, jnp.arange(N_GRP, dtype=jnp.int32))
    flat = indexes.reshape(-1)
    max_cos = jnp.zeros((rows,), jnp.float32).at[flat].set(bests.reshape(-1), mode='drop')
    log_mass = jnp.zeros((rows,), jnp.float32).at[flat].set(masses.reshape(-1), mode='drop')
    return (max_cos, log_mass)
```

```python
import functools

import jax
import jax.numpy as jnp
from jax import lax
from jax.experimental import pallas as pl
from jax.experimental.pallas import tpu as pltpu
from jax.sharding import PartitionSpec as P

MESH = pl.DeviceIdType.MESH
F32 = jnp.float32
BF16 = jnp.bfloat16
GROUPS = 8
SLOTS = 6
MASKED = -30.0
ORDER = (0, 1, 3, 2)

ZB, XB, CB = "z", "x", "c"


def program():
    steps = []

    def ev(*names):
        steps.extend(("ev", kind, q) for kind, qs in names for q in qs)

    def full(i, a, j, b):
        steps.append(("tile", i, a, j, b))

    def self_tile(a):
        steps.append(("self", a))

    ev(("E0", [0, 1]), ("E1", [0, 1]), ("E0", [2, 3]))
    self_tile(0)
    ev(("E1", [2]), ("E2", [0]), ("E0", [4, 5]), ("E2", [1]), ("E1", [3]))
    full(0, 0, 1, 0)
    ev(("E4", [0, 1, 2, 3]), ("E2", [2]), ("E1", [4]))
    ev(("E2", [3]), ("E1", [5]), ("E3", [0, 1, 2, 3]))
    full(3, 0, 1, 0)
    ev(("E2", [4]), ("E5", [0, 1, 2, 3]))
    full(3, 0, 4, 0)
    ev(("E2", [5]), ("E0", [6]))
    full(3, 0, 5, 0)
    ev(("E0", [7]), ("E1", [6]))
    self_tile(1)
    full(0, 0, 0, 1)
    ev(("E1", [7]), ("E2", [6]))
    full(0, 1, 1, 0)
    full(0, 1, 2, 0)
    ev(("E2", [7]))
    full(0, 1, 3, 0)
    full(0, 1, 5, 0)
    full(0, 1, 4, 0)
    ev(("E4", [4, 5, 6, 7]))
    full(0, 0, 1, 1)
    full(0, 1, 1, 1)
    full(3, 0, 1, 1)
    full(3, 0, 4, 1)
    full(0, CB, 4, CB)
    full(5, 0, 1, 1)
    ev(("E5", [4, 5, 6, 7]))
    full(0, ZB, 2, ZB)
    full(3, 0, 2, 1)
    full(3, 0, 5, 1)
    full(0, CB, 5, CB)
    full(5, 0, 2, 1)
    full(5, CB, 2, CB)
    full(5, CB, 1, CB)
    ev(("E3", [4, 5, 6, 7]))
    full(3, 1, 1, 0)
    full(3, 1, 1, 1)
    full(0, XB, 3, XB)
    full(3, XB, 2, XB)
    full(3, 1, 5, 0)
    full(3, 1, 5, 1)
    full(3, 1, 4, 0)
    full(3, 1, 4, 1)
    return steps


ROWSLOT = {0: 0, 3: 1, 5: 2}


def kernel(
    cap, cid_ref, cg_ref, emb_ref, best_ref, mass_ref,
    emb, unit, hot, outgo, sh, tagout, tagin, ct, rowtag,
    rowmax, rowsum, colmax, colsum, msg, rmsg, res, back, ids,
    in_sem, a_s, a_r, f_s, f_r, t_s, t_r, ct_s, ct_r, m_s, m_r, b_s, b_r,
):
    rows, width = emb.shape
    half = 4 * cap
    lanes = 128
    g, b = lax.axis_index("grp"), lax.axis_index("blk")
    y, c = g // 2, g % 2
    x, z = b // 4, b % 4
    h, xb = x // 2, x % 2
    xn = 2 * h + 1 - xb
    step = 2 * c - 1
    zf = (z + step + 4) % 4
    zb = (z - step + 4) % 4
    z2 = (z + 2) % 4
    x3 = 3 - x

    def dev(px, py, pz, pc):
        return {"grp": 2 * py + pc, "blk": 4 * px + pz}

    z3 = z + 2 * c - 4 * ((z + 2 * c) // 4)
    holder = {
        1: dev(x, y, zf, c), 2: dev(x, y, z2, c), 3: dev(xn, y, z3, c),
        4: dev(x, y, z, 1 - c), 5: dev(x, y, zf, 1 - c),
    }
    owner = dict(holder)
    owner[1] = dev(x, y, zb, c)

    barrier = pltpu.get_barrier_semaphore()
    friends = []
    for dy in range(4):
        yd = (y + dy) % 4
        for pc in (0, 1):
            if dy:
                friends.append(dev(x, yd, z, pc))
            friends.append(dev(x3, yd, z, pc))
    friends += [
        dev(x, y, z, 1 - c), dev(x, y, zf, c), dev(x, y, zb, c), dev(x, y, z2, c),
        dev(xn, y, z, c), dev(xn, y, z2, c), dev(x, y, zf, 1 - c),
    ]
    for d in friends:
        pl.semaphore_signal(barrier, inc=1, device_id=d, device_id_type=MESH)

    parts = 4
    size = rows // parts

    def load(k):
        return pltpu.make_async_copy(
            emb_ref.at[pl.ds(k * size, size)], emb.at[pl.ds(k * size, size)], in_sem.at[k]
        )

    for k in range(parts):
        load(k).start()

    plan = program()
    tiles = [s for s in plan if s[0] != "ev"]
    bits = {ZB: z // 2, XB: xb, CB: c}

    def pick(t, values):
        value = 0
        for k, (base, bit) in enumerate(values):
            value = jnp.where(t == k, base + (bits[bit] if bit in bits else bit), value)
        return value

    def operands(t):
        work = [s[1:] if s[0] == "tile" else (0, 0, 0, 0) for s in tiles]
        ri = pick(t, [(2 * ROWSLOT[i], a) for i, a, _, _ in work])
        i = ri + jnp.where(ri < 2, 0, jnp.where(ri < 4, 4, 6))
        j = pick(t, [(2 * j, a) for _, _, j, a in work])
        return ri, i, j

    cid = cid_ref[...]
    group = jnp.zeros(cid.shape, jnp.int32)
    for k in range(cg_ref.shape[0]):
        group = jnp.where(cid == k, cg_ref[k], group)
    dy = ((group >> 1) - y) & 3
    order = jnp.where(dy == 0, 0, jnp.where(dy == 1, 1, jnp.where(dy == 3, 2, 3)))
    other = jnp.where((group & 1) == h, 0, 1)
    target = 2 * order + other
    picks = jnp.where(
        lax.broadcasted_iota(jnp.int32, (GROUPS, rows), 0) == target, 1.0, 0.0
    ).astype(F32)
    earlier = jnp.where(
        lax.broadcasted_iota(jnp.int32, (rows, rows), 0)
        < lax.broadcasted_iota(jnp.int32, (rows, rows), 1),
        1.0,
        0.0,
    ).astype(BF16)
    before = jnp.dot(picks.astype(BF16), earlier, preferred_element_type=F32)
    rank = jnp.sum(picks * before, axis=0, keepdims=True).astype(jnp.int32)
    place = target * cap + rank
    hot[...] = jnp.where(
        lax.broadcasted_iota(jnp.int32, (GROUPS * cap, rows), 0) == place, 1.0, 0.0
    ).astype(BF16)
    ids[...] = jnp.zeros(ids.shape, jnp.int32)
    for k in range(rows // lanes):
        ids[0, k : k + 1, :] = target[:, k * lanes : (k + 1) * lanes]
        ids[1, k : k + 1, :] = rank[:, k * lanes : (k + 1) * lanes]

    names = jnp.broadcast_to((cid + 1).astype(F32), (8, rows)).astype(BF16)
    tags = lax.dot_general(
        names, hot[...], (((1,), (1,)), ((), ())), preferred_element_type=F32
    )
    tagout[...] = jnp.zeros(tagout.shape, F32)
    for k in range(GROUPS):
        tagout[k, :, 0:cap] = tags[:, k * cap : (k + 1) * cap]

    rowmax[...] = jnp.full(rowmax.shape, -1.0, F32)
    colmax[...] = jnp.full(colmax.shape, -1.0, F32)
    rowsum[...] = jnp.zeros(rowsum.shape, F32)
    colsum[...] = jnp.zeros(colsum.shape, F32)
    res[...] = jnp.zeros(res.shape, F32)
    msg[...] = jnp.zeros(msg.shape, F32)

    pl.semaphore_wait(barrier, len(friends))

    def chunk(slot, q):
        return sh.at[2 * slot + q // 4, pl.ds((q % 4) * cap, cap)]

    def dest(n):
        yd = (y + ORDER[n // 2]) % 4
        return dev(x, yd, z, 0) if n % 2 == 0 else dev(x3, yd, z, 1)

    def landing(n):
        q = 2 * (n // 2) + c
        return sh.at[(n // 2) // 2, pl.ds((2 * ((n // 2) % 2) + c) * cap, cap)], q

    def send_tag(n):
        q = 2 * (n // 2) + c
        return pltpu.make_async_remote_copy(
            tagout.at[n], tagin.at[q], t_s.at[n], t_r.at[q], device_id=dest(n), device_id_type=MESH
        )

    def send_rows(n):
        dst, q = landing(n)
        return pltpu.make_async_remote_copy(
            outgo.at[pl.ds(n * cap, cap)], dst, a_s.at[n], a_r.at[q],
            device_id=dest(n), device_id_type=MESH,
        )

    keep_tag = pltpu.make_async_copy(tagout.at[0], tagin.at[0], t_r.at[0])
    keep_rows = pltpu.make_async_copy(outgo.at[pl.ds(0, cap)], chunk(0, 0), a_r.at[0])

    def start(n, remote, local):
        if n:
            remote.start()
        else:
            pl.when(c == 0)(local.start)
            pl.when(c == 1)(remote.start)

    for n in range(GROUPS):
        start(n, send_tag(n), keep_tag)

    for k in range(parts):
        load(k).wait()
        v = emb[pl.ds(k * size, size)]
        scale = lax.rsqrt(jnp.sum(v * v, axis=1, keepdims=True) + 1e-06)
        unit[pl.ds(k * size, size)] = (v * scale).astype(BF16)
    for k in range(GROUPS // 2):
        outgo[pl.ds(2 * k * cap, 2 * cap)] = jnp.dot(
            hot[pl.ds(2 * k * cap, 2 * cap)], unit[...], preferred_element_type=F32
        ).astype(BF16)
        for n in (2 * k, 2 * k + 1):
            start(n, send_rows(n), keep_rows)

    def landed(ref, sem):
        pltpu.make_async_copy(ref, ref, sem).wait()

    for q in range(GROUPS):
        landed(tagin.at[q], t_r.at[q])
        ct[q // 4, :, (q % 4) * cap : (q % 4 + 1) * cap] = tagin[q, :, 0:cap]

    def send_ct(j):
        return pltpu.make_async_remote_copy(
            ct.at[pl.ds(0, 2)], ct.at[pl.ds(2 * j, 2)], ct_s.at[j - 1], ct_r.at[j - 1],
            device_id=holder[j], device_id_type=MESH,
        )

    for j in range(1, SLOTS):
        send_ct(j).start()

    def row_tags(slot):
        for a in (0, 1):
            for k in range(half // lanes):
                v = ct[2 * slot + a, 0:1, k * lanes : (k + 1) * lanes]
                v = jnp.where(v == 0.0, -1.0, v)
                rowtag[2 * ROWSLOT[slot] + a, pl.ds(k * lanes, lanes), :] = jnp.transpose(
                    jnp.broadcast_to(v, (lanes, lanes))
                )

    row_tags(0)
    for j in range(1, SLOTS):
        landed(ct.at[pl.ds(2 * j, 2)], ct_r.at[j - 1])
    row_tags(3)
    row_tags(5)

    def forward(src, slot, q, to):
        return pltpu.make_async_remote_copy(
            chunk(src, q), chunk(slot, q), f_s.at[slot - 1, q], f_r.at[slot - 1, q],
            device_id=to, device_id_type=MESH,
        )

    ahead, across, sibling = dev(x, y, zf, c), dev(xn, y, z, c), dev(x, y, z, 1 - c)

    def event(kind, q):
        slot = int(kind[1])
        sem = a_r.at[q] if slot == 0 else f_r.at[slot - 1, q]
        landed(chunk(slot, q), sem)
        if slot == 0:
            forward(0, 1, q, ahead).start()
            pl.when(c == 0)(forward(0, 3, q, across).start)
            forward(0, 4, q, sibling).start()
        if slot == 1:
            forward(1, 2, q, ahead).start()
            forward(1, 5, q, sibling).start()
        if slot == 2:
            pl.when(c == 1)(forward(2, 3, q, across).start)

    def cut(ref, k):
        return ref[:, k * lanes : (k + 1) * lanes]

    blocks = half // lanes

    def scores(i, j):
        return lax.dot_general(
            sh[i], sh[j], (((1,), (1,)), ((), ())), preferred_element_type=F32
        )

    def tile(ri, i, j):
        s = scores(i, j)
        cm = [colmax[j, :, k * lanes : (k + 1) * lanes] for k in range(blocks)]
        cs = [colsum[j, :, k * lanes : (k + 1) * lanes] for k in range(blocks)]
        tag = [ct[j, 0:1, k * lanes : (k + 1) * lanes] for k in range(blocks)]
        for r in range(blocks):
            at = slice(r * lanes, (r + 1) * lanes)
            rt, rm, rs = rowtag[ri, at, :], rowmax[ri, at, :], rowsum[ri, at, :]
            for k in range(blocks):
                v = jnp.where(rt == tag[k], s[at, k * lanes : (k + 1) * lanes], MASKED)
                e = jnp.exp(20.0 * v)
                rm, rs = jnp.maximum(rm, v), rs + e
                cm[k] = jnp.maximum(cm[k], jnp.max(v.reshape(lanes // 8, 8, lanes), axis=0))
                cs[k] = cs[k] + jnp.sum(e.reshape(lanes // 8, 8, lanes), axis=0)
            rowmax[ri, at, :], rowsum[ri, at, :] = rm, rs
        for k in range(blocks):
            colmax[j, :, k * lanes : (k + 1) * lanes] = cm[k]
            colsum[j, :, k * lanes : (k + 1) * lanes] = cs[k]

    def own_tile(a):
        s = scores(a, a)
        off = lax.broadcasted_iota(jnp.int32, (lanes, lanes), 0) != lax.broadcasted_iota(
            jnp.int32, (lanes, lanes), 1
        )
        for r in range(blocks):
            at = slice(r * lanes, (r + 1) * lanes)
            rt, rm, rs = rowtag[a, at, :], rowmax[a, at, :], rowsum[a, at, :]
            for k in range(blocks):
                hit = rt == ct[a, 0:1, k * lanes : (k + 1) * lanes]
                if r == k:
                    hit = hit & off
                v = jnp.where(hit, s[at, k * lanes : (k + 1) * lanes], MASKED)
                e = jnp.exp(20.0 * v)
                rm, rs = jnp.maximum(rm, v), rs + e
            rowmax[a, at, :], rowsum[a, at, :] = rm, rs

    events, selfs, count = {}, [], 0
    for s in plan:
        if s[0] == "ev":
            events.setdefault(count, []).append(s[1:])
        else:
            if s[0] == "self":
                selfs.append(count)
            count += 1

    def turn(t, carry):
        for when, what in events.items():

            @pl.when(t == when)
            def _(what=what):
                for kind, q in what:
                    event(kind, q)

        own = (t == selfs[0]) | (t == selfs[1])

        @pl.when(own)
        def _():
            own_tile(t // selfs[1])

        @pl.when(jnp.logical_not(own))
        def _():
            tile(*operands(t))

        return carry

    lax.fori_loop(0, count, turn, 0)

    def flat(ref, ri, k, op):
        return op(
            jnp.transpose(ref[ri, k * lanes : (k + 1) * lanes, :]), axis=0, keepdims=True
        )

    def collect(j):
        for a in (0, 1):
            top = jnp.max(colmax[2 * j + a], axis=0, keepdims=True)
            total = jnp.sum(colsum[2 * j + a], axis=0, keepdims=True)
            msg[2 * j + a, 0:1, :], msg[2 * j + a, 1:2, :] = top, total
            if j in ROWSLOT:
                ri = 2 * ROWSLOT[j] + a
                for k in range(blocks):
                    at = slice(k * lanes, (k + 1) * lanes)
                    msg[2 * j + a, 0:1, at] = jnp.maximum(
                        msg[2 * j + a, 0:1, at], flat(rowmax, ri, k, jnp.max)
                    )
                    msg[2 * j + a, 1:2, at] = msg[2 * j + a, 1:2, at] + flat(
                        rowsum, ri, k, jnp.sum
                    )

    def send_msg(j):
        return pltpu.make_async_remote_copy(
            msg.at[pl.ds(2 * j, 2)], rmsg.at[pl.ds(2 * j, 2)], m_s.at[j - 1], m_r.at[j - 1],
            device_id=owner[j], device_id_type=MESH,
        )

    for j in (3, 5, 2, 1, 4):
        collect(j)
        send_msg(j).start()
    collect(0)
    for j in range(1, SLOTS):
        landed(rmsg.at[pl.ds(2 * j, 2)], m_r.at[j - 1])
    for a in (0, 1):
        top, total = msg[a, 0:1, :], msg[a, 1:2, :]
        for j in range(1, SLOTS):
            top = jnp.maximum(top, rmsg[2 * j + a, 0:1, :])
            total = total + rmsg[2 * j + a, 1:2, :]
        mass = jnp.log(1.0 + total)
        for k in range(4):
            res[4 * a + k, 0:1, 0:cap] = top[:, k * cap : (k + 1) * cap]
            res[4 * a + k, 1:2, 0:cap] = mass[:, k * cap : (k + 1) * cap]

    def send_back(q):
        ys = (y - ORDER[q // 2] + 4) % 4
        xs = x + c * (x3 - x)
        n = 2 * (q // 2) + c
        return pltpu.make_async_remote_copy(
            res.at[q], back.at[n], b_s.at[q], b_r.at[n],
            device_id=dev(xs, ys, z, q % 2), device_id_type=MESH,
        )

    keep_back = pltpu.make_async_copy(res.at[0], back.at[0], b_r.at[0])
    for q in range(GROUPS):
        start(q, send_back(q), keep_back)
    for n in range(GROUPS):
        landed(back.at[n], b_r.at[n])

    target8, rank8 = ids[0], ids[1]
    outs = [jnp.zeros((8, lanes), F32), jnp.zeros((8, lanes), F32)]
    for n in range(GROUPS):
        for k in (0, 1):
            line = jnp.broadcast_to(back[n, k : k + 1, :], (8, lanes))
            found = jnp.take_along_axis(line, rank8, axis=1)
            outs[k] = jnp.where(target8 == n, found, outs[k])
    best_ref[...] = outs[0][0 : rows // lanes]
    mass_ref[...] = outs[1][0 : rows // lanes]

    def left(ref, sem):
        pltpu.make_async_copy(ref, ref, sem).wait()

    for n in range(GROUPS):
        if n:
            send_tag(n).wait_send()
            send_rows(n).wait_send()
            send_back(n).wait_send()
        else:
            pl.when(c == 1)(send_tag(n).wait_send)
            pl.when(c == 1)(send_rows(n).wait_send)
            pl.when(c == 1)(send_back(n).wait_send)
    for j in range(1, SLOTS):
        send_ct(j).wait_send()
        send_msg(j).wait_send()
    for q in range(GROUPS):
        forward(0, 1, q, ahead).wait_send()
        forward(0, 4, q, sibling).wait_send()
        forward(1, 2, q, ahead).wait_send()
        forward(1, 5, q, sibling).wait_send()
        forward(0, 3, q, across).wait_send()


def body(embeddings, cluster_id, cluster_group):
    rows, width = embeddings.shape
    cap = rows * 3 // (2 * GROUPS)
    half, lanes = 4 * cap, 128
    dma = pltpu.SemaphoreType.DMA
    out = jax.ShapeDtypeStruct((rows // lanes, lanes), F32)
    best, mass = pl.pallas_call(
        functools.partial(kernel, cap),
        out_shape=(out, out),
        in_specs=[
            pl.BlockSpec(memory_space=pltpu.VMEM),
            pl.BlockSpec(memory_space=pltpu.SMEM),
            pl.BlockSpec(memory_space=pl.ANY),
        ],
        out_specs=(
            pl.BlockSpec(memory_space=pltpu.VMEM),
            pl.BlockSpec(memory_space=pltpu.VMEM),
        ),
        scratch_shapes=[
            pltpu.VMEM((rows, width), F32),
            pltpu.VMEM((rows, width), BF16),
            pltpu.VMEM((GROUPS * cap, rows), BF16),
            pltpu.VMEM((GROUPS * cap, width), BF16),
            pltpu.VMEM((2 * SLOTS, half, width), BF16),
            pltpu.VMEM((GROUPS, 8, lanes), F32),
            pltpu.VMEM((GROUPS, 8, lanes), F32),
            pltpu.VMEM((2 * SLOTS, 8, half), F32),
            pltpu.VMEM((6, half, lanes), F32),
            pltpu.VMEM((6, half, lanes), F32),
            pltpu.VMEM((6, half, lanes), F32),
            pltpu.VMEM((2 * SLOTS, 8, half), F32),
            pltpu.VMEM((2 * SLOTS, 8, half), F32),
            pltpu.VMEM((2 * SLOTS, 8, half), F32),
            pltpu.VMEM((2 * SLOTS, 8, half), F32),
            pltpu.VMEM((GROUPS, 8, lanes), F32),
            pltpu.VMEM((GROUPS, 8, lanes), F32),
            pltpu.VMEM((2, 8, lanes), jnp.int32),
            dma((4,)),
            dma((GROUPS,)), dma((GROUPS,)),
            dma((SLOTS - 1, GROUPS)), dma((SLOTS - 1, GROUPS)),
            dma((GROUPS,)), dma((GROUPS,)),
            dma((SLOTS - 1,)), dma((SLOTS - 1,)),
            dma((SLOTS - 1,)), dma((SLOTS - 1,)),
            dma((GROUPS,)), dma((GROUPS,)),
        ],
        compiler_params=pltpu.CompilerParams(
            collective_id=0, has_side_effects=True, vmem_limit_bytes=48 * 2**20
        ),
    )(cluster_id.reshape(1, rows), cluster_group, embeddings)
    return best.reshape(rows), mass.reshape(rows)


def solution(mesh):
    in_specs = (P(("grp", "blk"), None), P(("grp", "blk")), P())
    out_specs = (P(("grp", "blk")), P(("grp", "blk")))
    return jax.shard_map(body, mesh=mesh, in_specs=in_specs, out_specs=out_specs, check_vma=False)
```

```python
import functools

import jax
import jax.numpy as jnp
from jax import lax
from jax.experimental import pallas as pl
from jax.experimental.pallas import tpu as pltpu
from jax.sharding import PartitionSpec as P

MESH = pl.DeviceIdType.MESH
F32 = jnp.float32
BF16 = jnp.bfloat16
GROUPS = 8
SLOTS = 6
MASKED = -30.0
SENDS = ((0, 0), (0, 1), (1, 0), (3, 0), (1, 1), (3, 1), (2, 0), (2, 1))

KINDS = {"n": 0, "w": 1, "s": 2}
SLOT_OF = {"E": 0, "F": 1, "G": 2, "K": 3, "D": 4, "H": 5}
PROGRAMS = (
    (
        "S1", "S2", "E0", "W2", "S3", "T0", "E2", "F0", "W1", "S4", "W3", "S6", "E1", "E3", "R0",
        ("s", 0, 0, 0, 0), "C4", "D0", "D1", "D2", "D3", ("n", 0, 0, 4, 0), "W4", "S5", "F2", "G0", "E4", "C3",
        "K0", "K1", "K2", "K3", "R3", ("n", 3, 0, 4, 0), "E6", "F1", "F3", "C1", ("n", 0, 0, 1, 0),
        ("n", 3, 0, 1, 0), "W5", "S7", "C5", "H0", "H1", "H2", "H3", ("n", 3, 0, 5, 0), ("n", 0, 0, 5, 0),
        "E5", "R5", ("n", 5, 0, 1, 0), "G2", "E7", ("s", 0, 1, 0, 1), "F4", ("n", 0, 0, 0, 1),
        ("n", 0, 1, 1, 0), "D4", "D5", "D6", "D7", ("n", 3, 0, 4, 1), ("n", 0, 1, 3, 0), "F6", "G1",
        ("n", 0, 1, 5, 0), "G3", "C2", ("n", 0, 1, 2, 0), ("n", 0, 1, 4, 0), "K4", "K5", "K6", "K7",
        ("w", 3, 1, 4, 0), "F5", ("n", 0, "x", 3, "x"), ("n", 5, 0, 2, 0), "F7", ("n", 0, 0, 1, 1), "G4",
        ("n", 0, 1, 1, 1), ("n", 3, 0, 1, 1), "G6", ("w", 3, 1, 1, 0), "H4", "H5", "H6", "H7",
        ("n", 3, 0, 5, 1), "G5", ("w", 3, 1, 5, 0), ("n", 5, 0, 1, 1), "G7", ("n", 0, "z", 2, "z"),
        ("n", 3, 0, 2, 1), ("n", 3, "x", 2, "x"), ("n", 5, 0, 2, 1),
    ),
    (
        "S1", "S3", "E0", "W3", "S2", "T0", "E3", "F0", "W1", "S5", "W2", "S6", "E1", "E2", "R0",
        ("s", 0, 0, 0, 0), "W5", "S4", "F3", "G0", "E5", "E6", "F1", "F2", "C1", ("n", 0, 0, 1, 0), "W4", "S7",
        "E4", "G3", "E7", ("s", 0, 1, 0, 1), "F5", ("n", 0, 0, 0, 1), ("n", 0, 1, 1, 0), "C5", "H0", "H1",
        "H2", "H3", ("n", 0, 1, 5, 0), "C4", "D0", "D1", "D2", "D3", ("n", 0, 1, 4, 0), "F6", "G1", "D4", "D5",
        "D6", "D7", ("n", 0, 1, 4, 1), "G2", "C2", ("n", 0, 1, 2, 0), "F4", "F7", ("n", 0, 0, 1, 1), "G5",
        ("n", 0, 1, 1, 1), "C3", "K0", "K1", "K2", "K3", "R3", ("n", 3, 0, 1, 0), "G6", ("n", 3, 0, 1, 1),
        ("n", 3, 0, 5, 0), "G4", "H4", "H5", "H6", "H7", ("n", 3, 0, 5, 1), ("n", 3, 0, 4, 0), "G7",
        ("n", 3, 0, 4, 1), ("n", 0, "z", 2, "z"), ("n", 0, 1, 3, 0), ("n", 3, 0, 2, 1), ("n", 0, 1, 5, 1),
        "R5", ("n", 5, 0, 2, 1), ("n", 5, 1, 2, 1), ("n", 5, 0, 1, 1), ("n", 5, 1, 1, 1), "K4", "K5", "K6",
        "K7", ("w", 3, 1, 1, 0), ("w", 3, 1, 5, 0), ("w", 3, 1, 4, 0), ("n", 0, "x", 3, "x"),
        ("n", 3, "x", 2, "x"),
    ),
)


ROWSLOT = {0: 0, 3: 1, 5: 2}


def kernel(
    cap, cid_ref, cg_ref, emb_ref, best_ref, mass_ref,
    emb, unit, hot, outgo, sh, tagout, tagin, ct, rowtag,
    rowmax, rowsum, colmax, colsum, msg, rmsg, res, back, ids,
    in_sem, a_s, a_r, f_s, f_r, t_s, t_r, ct_s, ct_r, m_s, m_r, b_s, b_r,
):
    rows, width = emb.shape
    half = 4 * cap
    lanes = 128
    g, b = lax.axis_index("grp"), lax.axis_index("blk")
    y, c = g // 2, g % 2
    x, z = b // 4, b % 4
    h, xb = x // 2, x % 2
    xn = 2 * h + 1 - xb
    step = 2 * c - 1
    zf = (z + step + 4) % 4
    zb = (z - step + 4) % 4
    z2 = (z + 2) % 4
    x3 = 3 - x

    def dev(px, py, pz, pc):
        return {"grp": 2 * py + pc, "blk": 4 * px + pz}

    z3 = z + 2 * c - 4 * ((z + 2 * c) // 4)
    holder = {
        1: dev(x, y, zf, c), 2: dev(x, y, z2, c), 3: dev(xn, y, z3, c),
        4: dev(x, y, z, 1 - c), 5: dev(x, y, zf, 1 - c),
    }
    owner = dict(holder)
    owner[1] = dev(x, y, zb, c)

    barrier = pltpu.get_barrier_semaphore()
    friends = []
    for dy in range(4):
        if dy:
            friends.append(dev(x, (y + dy) % 4, z, c))
        friends.append(dev(x3, (y + dy) % 4, z, c))
    friends += [
        dev(x, y, z, 1 - c), dev(x, y, zf, c), dev(x, y, zb, c), dev(x, y, z2, c),
        dev(xn, y, z, c), dev(xn, y, z2, c), dev(x, y, zf, 1 - c),
    ]
    for d in friends:
        pl.semaphore_signal(barrier, inc=1, device_id=d, device_id_type=MESH)

    parts = 4
    size = rows // parts

    def load(k):
        return pltpu.make_async_copy(
            emb_ref.at[pl.ds(k * size, size)], emb.at[pl.ds(k * size, size)], in_sem.at[k]
        )

    for k in range(parts):
        load(k).start()

    events, tiles = [], []
    for plan in PROGRAMS:
        when, work = {}, []
        for item in plan:
            if isinstance(item, str):
                when.setdefault(len(work), []).append((item[0], int(item[1])))
            else:
                work.append(item)
        events.append(when)
        tiles.append(work)
    count = len(tiles[0])
    bits = {"z": z // 2, "x": xb}

    def number(item):
        kind, i, a, j, b = item
        base = 256 * KINDS[kind] + 16 * (2 * j) + 2 * i
        if a in bits:
            return base, a
        return base + a + 16 * b, None

    words = []
    for k in range(0, count, 3):
        both = []
        for work in tiles:
            word = 0
            for r, item in enumerate(work[k : k + 3]):
                base, bit = number(item)
                word = word + base * 1024**r
                if bit is not None:
                    word = word + bits[bit] * (17 * 1024**r)
            both.append(word)
        words.append(jnp.where(c == 0, both[0], both[1]))

    def operands(t):
        u, r = t // 3, t % 3
        word = words[0]
        for k in range(1, len(words)):
            word = jnp.where(u == k, words[k], word)
        code = jnp.where(r == 0, word, jnp.where(r == 1, word // 1024, word // 1024**2)) % 1024
        kind, j, i = code // 256, code // 16 % 16, code % 16
        return kind, i - jnp.where(i < 2, 0, jnp.where(i < 8, 4, 6)), i, j

    cid = cid_ref[...]
    group = jnp.zeros(cid.shape, jnp.int32)
    for k in range(cg_ref.shape[0]):
        group = jnp.where(cid == k, cg_ref[k], group)
    dy = ((group >> 1) - y) & 3
    other = (group & 1) ^ h
    target = jnp.zeros(cid.shape, jnp.int32)
    for n, (sy, sx) in enumerate(SENDS):
        target = jnp.where((dy == sy) & (other == sx), n, target)
    picks = jnp.where(
        lax.broadcasted_iota(jnp.int32, (GROUPS, rows), 0) == target, 1.0, 0.0
    ).astype(F32)
    earlier = jnp.where(
        lax.broadcasted_iota(jnp.int32, (rows, rows), 0)
        < lax.broadcasted_iota(jnp.int32, (rows, rows), 1),
        1.0,
        0.0,
    ).astype(BF16)
    before = jnp.dot(picks.astype(BF16), earlier, preferred_element_type=F32)
    rank = jnp.sum(picks * before, axis=0, keepdims=True).astype(jnp.int32)
    place = target * cap + rank
    hot[...] = jnp.where(
        lax.broadcasted_iota(jnp.int32, (GROUPS * cap, rows), 0) == place, 1.0, 0.0
    ).astype(BF16)
    ids[...] = jnp.zeros(ids.shape, jnp.int32)
    for k in range(rows // lanes):
        ids[0, k : k + 1, :] = target[:, k * lanes : (k + 1) * lanes]
        ids[1, k : k + 1, :] = rank[:, k * lanes : (k + 1) * lanes]

    names = jnp.broadcast_to((cid + 1).astype(F32), (8, rows)).astype(BF16)
    tags = lax.dot_general(
        names, hot[...], (((1,), (1,)), ((), ())), preferred_element_type=F32
    )
    tagout[...] = jnp.zeros(tagout.shape, F32)
    for k in range(GROUPS):
        tagout[k, :, 0:cap] = tags[:, k * cap : (k + 1) * cap]

    rowmax[...] = jnp.full(rowmax.shape, -1.0, F32)
    colmax[...] = jnp.full(colmax.shape, -1.0, F32)
    rowsum[...] = jnp.zeros(rowsum.shape, F32)
    colsum[...] = jnp.zeros(colsum.shape, F32)
    res[...] = jnp.zeros(res.shape, F32)
    msg[...] = jnp.zeros(msg.shape, F32)

    for k in range(parts):
        load(k).wait()
        v = emb[pl.ds(k * size, size)]
        scale = lax.rsqrt(jnp.sum(v * v, axis=1, keepdims=True) + 1e-06)
        unit[pl.ds(k * size, size)] = (v * scale).astype(BF16)
    packed = jnp.dot(hot[...], unit[...], preferred_element_type=F32).astype(BF16)
    sh[0, 0:cap] = packed[0:cap]
    outgo[...] = packed

    pl.semaphore_wait(barrier, len(friends))

    def chunk(slot, q):
        return sh.at[2 * slot + q // 4, pl.ds((q % 4) * cap, cap)]

    def dest(n):
        sy, sx = SENDS[n]
        return dev(x3 if sx else x, (y + sy) % 4, z, c)

    def send_tag(n):
        return pltpu.make_async_remote_copy(
            tagout.at[n], tagin.at[n], t_s.at[n], t_r.at[n], device_id=dest(n), device_id_type=MESH
        )

    def send_rows(n):
        return pltpu.make_async_remote_copy(
            outgo.at[pl.ds(n * cap, cap)], chunk(0, n), a_s.at[n], a_r.at[n],
            device_id=dest(n), device_id_type=MESH,
        )

    for n in range(1, GROUPS):
        send_tag(n).start()

    def landed(ref, sem):
        pltpu.make_async_copy(ref, ref, sem).wait()

    def send_ct(j):
        return pltpu.make_async_remote_copy(
            ct.at[pl.ds(0, 2)], ct.at[pl.ds(2 * j, 2)], ct_s.at[j - 1], ct_r.at[j - 1],
            device_id=holder[j], device_id_type=MESH,
        )

    def own_tags():
        for q in range(GROUPS):
            if q:
                landed(tagin.at[q], t_r.at[q])
            tag = tagin if q else tagout
            ct[q // 4, :, (q % 4) * cap : (q % 4 + 1) * cap] = tag[q, :, 0:cap]
        for j in range(1, SLOTS):
            send_ct(j).start()

    def row_tags(slot):
        for a in (0, 1):
            for k in range(half // lanes):
                v = ct[2 * slot + a, 0:1, k * lanes : (k + 1) * lanes]
                v = jnp.where(v == 0.0, -1.0, v)
                rowtag[2 * ROWSLOT[slot] + a, pl.ds(k * lanes, lanes), :] = jnp.transpose(
                    jnp.broadcast_to(v, (lanes, lanes))
                )

    def forward(src, slot, q, to):
        return pltpu.make_async_remote_copy(
            chunk(src, q), chunk(slot, q), f_s.at[slot - 1, q], f_r.at[slot - 1, q],
            device_id=to, device_id_type=MESH,
        )

    ahead, across, sibling = dev(x, y, zf, c), dev(xn, y, z, c), dev(x, y, z, 1 - c)

    def event(kind, q):
        if kind == "T":
            return own_tags()
        if kind == "R":
            return row_tags(q)
        if kind == "C":
            return landed(ct.at[pl.ds(2 * q, 2)], ct_r.at[q - 1])
        if kind == "S":
            return send_rows(q).start()
        if kind == "W":
            return send_rows(q).wait_send()
        slot = SLOT_OF[kind]
        sem = a_r.at[q] if slot == 0 else f_r.at[slot - 1, q]
        if slot or q:
            landed(chunk(slot, q), sem)
        if slot == 0:
            forward(0, 1, q, ahead).start()
            pl.when(c == 0)(forward(0, 3, q, across).start)
            forward(0, 4, q, sibling).start()
        if slot == 1:
            forward(1, 2, q, ahead).start()
            forward(1, 5, q, sibling).start()
        if slot == 2:
            pl.when(c == 1)(forward(2, 3, q, across).start)

    def cut(ref, k):
        return ref[:, k * lanes : (k + 1) * lanes]

    blocks = half // lanes

    def scores(i, j):
        return lax.dot_general(
            sh[i], j, (((1,), (1,)), ((), ())), preferred_element_type=F32
        )

    def tile(ri, i, j, halves):
        s = scores(i, sh[pl.ds(j, halves)].reshape(halves * half, width))
        cols = [(j + a, slice(k * lanes, (k + 1) * lanes)) for a in range(halves) for k in range(blocks)]
        cm = [colmax[n, :, at] for n, at in cols]
        cs = [colsum[n, :, at] for n, at in cols]
        tag = [ct[n, 0:1, at] for n, at in cols]
        for r in range(blocks):
            at = slice(r * lanes, (r + 1) * lanes)
            rt, rm, rs = rowtag[ri, at, :], rowmax[ri, at, :], rowsum[ri, at, :]
            for k in range(len(cols)):
                v = jnp.where(rt == tag[k], s[at, k * lanes : (k + 1) * lanes], MASKED)
                e = jnp.exp(20.0 * v)
                rm, rs = jnp.maximum(rm, v), rs + e
                cm[k] = jnp.maximum(cm[k], jnp.max(v.reshape(lanes // 8, 8, lanes), axis=0))
                cs[k] = cs[k] + jnp.sum(e.reshape(lanes // 8, 8, lanes), axis=0)
            rowmax[ri, at, :], rowsum[ri, at, :] = rm, rs
        for k, (n, at) in enumerate(cols):
            colmax[n, :, at], colsum[n, :, at] = cm[k], cs[k]

    def own_tile(a):
        s = scores(a, sh[a])
        off = lax.broadcasted_iota(jnp.int32, (lanes, lanes), 0) != lax.broadcasted_iota(
            jnp.int32, (lanes, lanes), 1
        )
        for r in range(blocks):
            at = slice(r * lanes, (r + 1) * lanes)
            rt, rm, rs = rowtag[a, at, :], rowmax[a, at, :], rowsum[a, at, :]
            for k in range(blocks):
                hit = rt == ct[a, 0:1, k * lanes : (k + 1) * lanes]
                if r == k:
                    hit = hit & off
                v = jnp.where(hit, s[at, k * lanes : (k + 1) * lanes], MASKED)
                e = jnp.exp(20.0 * v)
                rm, rs = jnp.maximum(rm, v), rs + e
            rowmax[a, at, :], rowsum[a, at, :] = rm, rs

    group_of = 6

    def turn(t, carry):
        for first in range(0, count, group_of):

            @pl.when(t // group_of == first // group_of)
            def _(first=first):
                for k in range(first, min(first + group_of, count)):
                    for core in (0, 1):
                        what = events[core].get(k, [])
                        if what:

                            @pl.when((t == k) & (c == core))
                            def _(what=what):
                                for kind, q in what:
                                    event(kind, q)

        kind, ri, i, j = operands(t)

        @pl.when(kind == 0)
        def _():
            tile(ri, i, j, 1)

        @pl.when(kind == 1)
        def _():
            tile(ri, i, j, 2)

        @pl.when(kind == 2)
        def _():
            own_tile(ri)

        return carry

    lax.fori_loop(0, count, turn, 0)

    def flat(ref, ri, k, op):
        return op(
            jnp.transpose(ref[ri, k * lanes : (k + 1) * lanes, :]), axis=0, keepdims=True
        )

    def collect(j):
        for a in (0, 1):
            top = jnp.max(colmax[2 * j + a], axis=0, keepdims=True)
            total = jnp.sum(colsum[2 * j + a], axis=0, keepdims=True)
            msg[2 * j + a, 0:1, :], msg[2 * j + a, 1:2, :] = top, total
            if j in ROWSLOT:
                ri = 2 * ROWSLOT[j] + a
                for k in range(blocks):
                    at = slice(k * lanes, (k + 1) * lanes)
                    msg[2 * j + a, 0:1, at] = jnp.maximum(
                        msg[2 * j + a, 0:1, at], flat(rowmax, ri, k, jnp.max)
                    )
                    msg[2 * j + a, 1:2, at] = msg[2 * j + a, 1:2, at] + flat(
                        rowsum, ri, k, jnp.sum
                    )

    def send_msg(j):
        return pltpu.make_async_remote_copy(
            msg.at[pl.ds(2 * j, 2)], rmsg.at[pl.ds(2 * j, 2)], m_s.at[j - 1], m_r.at[j - 1],
            device_id=owner[j], device_id_type=MESH,
        )

    for j in (3, 5, 2, 1, 4):
        collect(j)
        send_msg(j).start()
    collect(0)
    for j in range(1, SLOTS):
        landed(rmsg.at[pl.ds(2 * j, 2)], m_r.at[j - 1])
    for a in (0, 1):
        top, total = msg[a, 0:1, :], msg[a, 1:2, :]
        for j in range(1, SLOTS):
            top = jnp.maximum(top, rmsg[2 * j + a, 0:1, :])
            total = total + rmsg[2 * j + a, 1:2, :]
        mass = jnp.log(1.0 + total)
        for k in range(4):
            res[4 * a + k, 0:1, 0:cap] = top[:, k * cap : (k + 1) * cap]
            res[4 * a + k, 1:2, 0:cap] = mass[:, k * cap : (k + 1) * cap]

    def send_back(q):
        sy, sx = SENDS[q]
        return pltpu.make_async_remote_copy(
            res.at[q], back.at[q], b_s.at[q], b_r.at[q],
            device_id=dev(x3 if sx else x, (y - sy + 4) % 4, z, c), device_id_type=MESH,
        )

    for q in range(1, GROUPS):
        send_back(q).start()
    for n in range(1, GROUPS):
        landed(back.at[n], b_r.at[n])

    target8, rank8 = ids[0], ids[1]
    outs = [jnp.zeros((8, lanes), F32), jnp.zeros((8, lanes), F32)]
    for n in range(GROUPS):
        for k in (0, 1):
            line = jnp.broadcast_to((back if n else res)[n, k : k + 1, :], (8, lanes))
            found = jnp.take_along_axis(line, rank8, axis=1)
            outs[k] = jnp.where(target8 == n, found, outs[k])
    best_ref[...] = outs[0][0 : rows // lanes]
    mass_ref[...] = outs[1][0 : rows // lanes]

    for n in range(1, GROUPS):
        send_tag(n).wait_send()
        send_back(n).wait_send()
        for core in (0, 1):
            if ("W", n) not in sum(events[core].values(), []):
                pl.when(c == core)(send_rows(n).wait_send)
    for j in range(1, SLOTS):
        send_ct(j).wait_send()
        send_msg(j).wait_send()
    for q in range(GROUPS):
        forward(0, 1, q, ahead).wait_send()
        forward(0, 4, q, sibling).wait_send()
        forward(1, 2, q, ahead).wait_send()
        forward(1, 5, q, sibling).wait_send()
        forward(0, 3, q, across).wait_send()


def body(embeddings, cluster_id, cluster_group):
    rows, width = embeddings.shape
    cap = rows * 3 // (2 * GROUPS)
    half, lanes = 4 * cap, 128
    dma = pltpu.SemaphoreType.DMA
    out = jax.ShapeDtypeStruct((rows // lanes, lanes), F32)
    best, mass = pl.pallas_call(
        functools.partial(kernel, cap),
        out_shape=(out, out),
        in_specs=[
            pl.BlockSpec(memory_space=pltpu.VMEM),
            pl.BlockSpec(memory_space=pltpu.SMEM),
            pl.BlockSpec(memory_space=pl.ANY),
        ],
        out_specs=(
            pl.BlockSpec(memory_space=pltpu.VMEM),
            pl.BlockSpec(memory_space=pltpu.VMEM),
        ),
        scratch_shapes=[
            pltpu.VMEM((rows, width), F32),
            pltpu.VMEM((rows, width), BF16),
            pltpu.VMEM((GROUPS * cap, rows), BF16),
            pltpu.VMEM((GROUPS * cap, width), BF16),
            pltpu.VMEM((2 * SLOTS, half, width), BF16),
            pltpu.VMEM((GROUPS, 8, lanes), F32),
            pltpu.VMEM((GROUPS, 8, lanes), F32),
            pltpu.VMEM((2 * SLOTS, 8, half), F32),
            pltpu.VMEM((6, half, lanes), F32),
            pltpu.VMEM((6, half, lanes), F32),
            pltpu.VMEM((6, half, lanes), F32),
            pltpu.VMEM((2 * SLOTS, 8, half), F32),
            pltpu.VMEM((2 * SLOTS, 8, half), F32),
            pltpu.VMEM((2 * SLOTS, 8, half), F32),
            pltpu.VMEM((2 * SLOTS, 8, half), F32),
            pltpu.VMEM((GROUPS, 8, lanes), F32),
            pltpu.VMEM((GROUPS, 8, lanes), F32),
            pltpu.VMEM((2, 8, lanes), jnp.int32),
            dma((4,)),
            dma((GROUPS,)), dma((GROUPS,)),
            dma((SLOTS - 1, GROUPS)), dma((SLOTS - 1, GROUPS)),
            dma((GROUPS,)), dma((GROUPS,)),
            dma((SLOTS - 1,)), dma((SLOTS - 1,)),
            dma((SLOTS - 1,)), dma((SLOTS - 1,)),
            dma((GROUPS,)), dma((GROUPS,)),
        ],
        compiler_params=pltpu.CompilerParams(
            collective_id=0, has_side_effects=True, vmem_limit_bytes=60 * 2**20
        ),
    )(cluster_id.reshape(1, rows), cluster_group, embeddings)
    return best.reshape(rows), mass.reshape(rows)


def solution(mesh):
    in_specs = (P(("grp", "blk"), None), P(("grp", "blk")), P())
    out_specs = (P(("grp", "blk")), P(("grp", "blk")))
    return jax.shard_map(body, mesh=mesh, in_specs=in_specs, out_specs=out_specs, check_vma=False)
```

```python
import functools

import jax
import jax.numpy as jnp
from jax import lax
from jax.experimental import pallas as pl
from jax.experimental.pallas import tpu as pltpu
from jax.sharding import PartitionSpec as P

MESH = pl.DeviceIdType.MESH
F32 = jnp.float32
BF16 = jnp.bfloat16
GROUPS = 8
SLOTS = 6
MASKED = -30.0
SENDS = ((0, 0), (0, 1), (1, 0), (3, 0), (1, 1), (3, 1), (2, 0), (2, 1))

KINDS = {"n": 0, "w": 1, "s": 2}
SLOT_OF = {"E": 0, "F": 1, "G": 2, "K": 3, "D": 4, "H": 5}
PROGRAMS = (
    (
        "S1", "S2", "S3", "E0", "T0", "F0", "W1", "W2", "W3", "S4", "S5", "E1", "E2", "E3", "R0",
        ("s", 0, 0, 0, 0), "C4", "D0", "D1", "D2", "D3", ("n", 0, 0, 4, 0), "W4", "W5", "S6", "S7", "F1", "F2",
        "F3", "C1", ("n", 0, 0, 1, 0), "E4", "E5", "C3", "K0", "K1", "K2", "K3", "R3", ("n", 3, 0, 1, 0), "C5",
        "H0", "H1", "H2", "H3", ("n", 3, 0, 5, 0), ("n", 3, 0, 4, 0), ("n", 0, 0, 5, 0), "R5",
        ("n", 5, 0, 1, 0), "E6", "E7", ("s", 0, 1, 0, 1), ("n", 0, 0, 0, 1), ("n", 0, 1, 1, 0), "D4", "D5",
        "D6", "D7", ("n", 3, 0, 4, 1), "F4", "F5", "C2", "G0", "G1", "G2", "G3", ("n", 0, 1, 2, 0),
        ("n", 0, 1, 3, 0), ("n", 0, 1, 5, 0), ("n", 0, 1, 4, 0), ("n", 5, 0, 2, 0), "F6", "F7",
        ("n", 0, 0, 1, 1), ("n", 0, 1, 1, 1), ("n", 3, 0, 1, 1), "K4", "K5", "K6", "K7", ("w", 3, 1, 1, 0),
        "H4", "H5", "H6", "H7", ("n", 3, 0, 5, 1), ("w", 3, 1, 5, 0), ("w", 3, 1, 4, 0), ("n", 0, "x", 3, "x"),
        ("n", 5, 0, 1, 1), "G4", "G5", "G6", "G7", ("n", 0, "z", 2, "z"), ("n", 3, 0, 2, 1),
        ("n", 3, "x", 2, "x"), ("n", 5, 0, 2, 1),
    ),
    (
        "S1", "S2", "S3", "E0", "T0", "F0", "W1", "W2", "W3", "S4", "S5", "E1", "E2", "E3", "R0",
        ("s", 0, 0, 0, 0), "G0", "W4", "W5", "S6", "S7", "F1", "F2", "F3", "C1", ("n", 0, 0, 1, 0), "E4", "E5",
        "E6", "E7", ("s", 0, 1, 0, 1), ("n", 0, 0, 0, 1), "G1", "G2", "G3", ("n", 0, 1, 1, 0), "C2",
        ("n", 0, 1, 2, 0), "F4", "F5", "C5", "H0", "H1", "H2", "H3", ("n", 0, 1, 5, 0), "C4", "D0", "D1", "D2",
        "D3", ("n", 0, 1, 4, 0), "D4", "D5", "D6", "D7", ("n", 0, 1, 4, 1), "F6", "F7", ("n", 0, 0, 1, 1),
        ("n", 0, 1, 1, 1), "R5", ("n", 5, 0, 1, 1), "H4", "H5", "H6", "H7", ("n", 0, 1, 5, 1),
        ("n", 5, 1, 1, 1), "G4", "G5", "C3", "K0", "K1", "K2", "K3", "R3", ("n", 3, 0, 1, 0),
        ("n", 3, 0, 1, 1), ("n", 3, 0, 5, 0), ("n", 3, 0, 5, 1), "G6", "G7", ("n", 3, 0, 4, 0),
        ("n", 3, 0, 4, 1), ("n", 0, "z", 2, "z"), ("n", 0, 1, 3, 0), ("n", 3, 0, 2, 1), ("n", 5, 0, 2, 1),
        ("n", 5, 1, 2, 1), "K4", "K5", "K6", "K7", ("w", 3, 1, 1, 0), ("w", 3, 1, 5, 0), ("w", 3, 1, 4, 0),
        ("n", 0, "x", 3, "x"), ("n", 3, "x", 2, "x"),
    ),
)


ROWSLOT = {0: 0, 3: 1, 5: 2}


def kernel(
    cap, cid_ref, cg_ref, emb_ref, out_ref,
    emb, unit, hot, outgo, sh, tagout, tagin, ct, rowtag,
    rowmax, rowsum, colmax, colsum, part, back, ids,
    in_sem, a_s, a_r, f_s, f_r, t_s, t_r, ct_s, ct_r, b_s, b_r,
):
    rows, width = emb.shape
    half = 4 * cap
    lanes = 128
    g, b = lax.axis_index("grp"), lax.axis_index("blk")
    y, c = g // 2, g % 2
    x, z = b // 4, b % 4
    h, xb = x // 2, x % 2
    xn = 2 * h + 1 - xb
    step = 2 * c - 1
    zf = (z + step + 4) % 4
    zb = (z - step + 4) % 4
    z2 = (z + 2) % 4
    x3 = 3 - x

    def dev(px, py, pz, pc):
        return {"grp": 2 * py + pc, "blk": 4 * px + pz}

    z3 = z + 2 * c - 4 * ((z + 2 * c) // 4)
    holder = {
        1: dev(x, y, zf, c), 2: dev(x, y, z2, c), 3: dev(xn, y, z3, c),
        4: dev(x, y, z, 1 - c), 5: dev(x, y, zf, 1 - c),
    }
    owner = dict(holder)
    owner[1] = dev(x, y, zb, c)

    barrier = pltpu.get_barrier_semaphore()
    friends = []
    for dy in range(4):
        if dy:
            friends.append(dev(x, (y + dy) % 4, z, c))
        friends.append(dev(x3, (y + dy) % 4, z, c))
    friends += [
        dev(x, y, z, 1 - c), dev(x, y, zf, c), dev(x, y, zb, c), dev(x, y, z2, c),
        dev(xn, y, z, c), dev(xn, y, z2, c), dev(x, y, zf, 1 - c),
    ]
    for d in friends:
        pl.semaphore_signal(barrier, inc=1, device_id=d, device_id_type=MESH)

    parts = 4
    size = rows // parts

    def load(k):
        return pltpu.make_async_copy(
            emb_ref.at[pl.ds(k * size, size)], emb.at[pl.ds(k * size, size)], in_sem.at[k]
        )

    for k in range(parts):
        load(k).start()

    events, tiles = [], []
    for plan in PROGRAMS:
        when, work = {}, []
        for item in plan:
            if isinstance(item, str):
                when.setdefault(len(work), []).append((item[0], int(item[1])))
            else:
                work.append(item)
        events.append(when)
        tiles.append(work)
    count = len(tiles[0])
    bits = {"z": z // 2, "x": xb}

    def number(item):
        kind, i, a, j, b = item
        base = 256 * KINDS[kind] + 16 * (2 * j) + 2 * i
        if a in bits:
            return base, a
        return base + a + 16 * b, None

    words = []
    for k in range(0, count, 3):
        both = []
        for work in tiles:
            word = 0
            for r, item in enumerate(work[k : k + 3]):
                base, bit = number(item)
                word = word + base * 1024**r
                if bit is not None:
                    word = word + bits[bit] * (17 * 1024**r)
            both.append(word)
        words.append(jnp.where(c == 0, both[0], both[1]))

    def operands(t):
        u, r = t // 3, t % 3
        word = words[0]
        for k in range(1, len(words)):
            word = jnp.where(u == k, words[k], word)
        code = jnp.where(r == 0, word, jnp.where(r == 1, word // 1024, word // 1024**2)) % 1024
        kind, j, i = code // 256, code // 16 % 16, code % 16
        return kind, i - jnp.where(i < 2, 0, jnp.where(i < 8, 4, 6)), i, j

    cid = cid_ref[...]
    group = jnp.zeros(cid.shape, jnp.int32)
    for k in range(cg_ref.shape[0]):
        group = jnp.where(cid == k, cg_ref[k], group)
    dy = ((group >> 1) - y) & 3
    other = (group & 1) ^ h
    target = jnp.zeros(cid.shape, jnp.int32)
    for n, (sy, sx) in enumerate(SENDS):
        target = jnp.where((dy == sy) & (other == sx), n, target)
    picks = jnp.where(
        lax.broadcasted_iota(jnp.int32, (GROUPS, rows), 0) == target, 1.0, 0.0
    ).astype(F32)
    earlier = jnp.where(
        lax.broadcasted_iota(jnp.int32, (rows, rows), 0)
        < lax.broadcasted_iota(jnp.int32, (rows, rows), 1),
        1.0,
        0.0,
    ).astype(BF16)
    before = jnp.dot(picks.astype(BF16), earlier, preferred_element_type=F32)
    rank = jnp.sum(picks * before, axis=0, keepdims=True).astype(jnp.int32)
    place = target * cap + rank
    hot[...] = jnp.where(
        lax.broadcasted_iota(jnp.int32, (GROUPS * cap, rows), 0) == place, 1.0, 0.0
    ).astype(BF16)
    ids[...] = jnp.zeros(ids.shape, jnp.int32)
    for k in range(rows // lanes):
        ids[0, k : k + 1, :] = target[:, k * lanes : (k + 1) * lanes]
        ids[1, k : k + 1, :] = rank[:, k * lanes : (k + 1) * lanes]

    names = jnp.broadcast_to((cid + 1).astype(F32), (8, rows)).astype(BF16)
    tags = lax.dot_general(
        names, hot[...], (((1,), (1,)), ((), ())), preferred_element_type=F32
    )
    tagout[...] = jnp.zeros(tagout.shape, F32)
    for k in range(GROUPS):
        tagout[k, :, 0:cap] = tags[:, k * cap : (k + 1) * cap]

    rowmax[...] = jnp.full(rowmax.shape, -1.0, F32)
    colmax[...] = jnp.full(colmax.shape, -1.0, F32)
    rowsum[...] = jnp.zeros(rowsum.shape, F32)
    colsum[...] = jnp.zeros(colsum.shape, F32)
    part[...] = jnp.zeros(part.shape, F32)

    for k in range(parts):
        load(k).wait()
        v = emb[pl.ds(k * size, size)]
        scale = lax.rsqrt(jnp.sum(v * v, axis=1, keepdims=True) + 1e-06)
        unit[pl.ds(k * size, size)] = (v * scale).astype(BF16)
    packed = jnp.dot(hot[...], unit[...], preferred_element_type=F32).astype(BF16)
    sh[0, 0:cap] = packed[0:cap]
    outgo[...] = packed

    pl.semaphore_wait(barrier, len(friends))

    def chunk(slot, q):
        return sh.at[2 * slot + q // 4, pl.ds((q % 4) * cap, cap)]

    def dest(n):
        sy, sx = SENDS[n]
        return dev(x3 if sx else x, (y + sy) % 4, z, c)

    def send_tag(n):
        return pltpu.make_async_remote_copy(
            tagout.at[n], tagin.at[n], t_s.at[n], t_r.at[n], device_id=dest(n), device_id_type=MESH
        )

    def send_rows(n):
        return pltpu.make_async_remote_copy(
            outgo.at[pl.ds(n * cap, cap)], chunk(0, n), a_s.at[n], a_r.at[n],
            device_id=dest(n), device_id_type=MESH,
        )

    for n in range(1, GROUPS):
        send_tag(n).start()

    def landed(ref, sem):
        pltpu.make_async_copy(ref, ref, sem).wait()

    def send_ct(j):
        return pltpu.make_async_remote_copy(
            ct.at[pl.ds(0, 2)], ct.at[pl.ds(2 * j, 2)], ct_s.at[j - 1], ct_r.at[j - 1],
            device_id=holder[j], device_id_type=MESH,
        )

    def own_tags():
        for q in range(GROUPS):
            if q:
                landed(tagin.at[q], t_r.at[q])
            tag = tagin if q else tagout
            ct[q // 4, :, (q % 4) * cap : (q % 4 + 1) * cap] = tag[q, :, 0:cap]
        for j in range(1, SLOTS):
            send_ct(j).start()

    def row_tags(slot):
        for a in (0, 1):
            for k in range(half // lanes):
                v = ct[2 * slot + a, 0:1, k * lanes : (k + 1) * lanes]
                v = jnp.where(v == 0.0, -1.0, v)
                rowtag[2 * ROWSLOT[slot] + a, pl.ds(k * lanes, lanes), :] = jnp.transpose(
                    jnp.broadcast_to(v, (lanes, lanes))
                )

    def forward(src, slot, q, to):
        return pltpu.make_async_remote_copy(
            chunk(src, q), chunk(slot, q), f_s.at[slot - 1, q], f_r.at[slot - 1, q],
            device_id=to, device_id_type=MESH,
        )

    ahead, across, sibling = dev(x, y, zf, c), dev(xn, y, z, c), dev(x, y, z, 1 - c)

    def event(kind, q):
        if kind == "T":
            return own_tags()
        if kind == "R":
            return row_tags(q)
        if kind == "C":
            return landed(ct.at[pl.ds(2 * q, 2)], ct_r.at[q - 1])
        if kind == "S":
            return send_rows(q).start()
        if kind == "W":
            return send_rows(q).wait_send()
        slot = SLOT_OF[kind]
        sem = a_r.at[q] if slot == 0 else f_r.at[slot - 1, q]
        if slot or q:
            landed(chunk(slot, q), sem)
        if slot == 0:
            forward(0, 1, q, ahead).start()
            pl.when(c == 0)(forward(0, 3, q, across).start)
            forward(0, 4, q, sibling).start()
        if slot == 1:
            forward(1, 2, q, ahead).start()
            forward(1, 5, q, sibling).start()
        if slot == 2:
            pl.when(c == 1)(forward(2, 3, q, across).start)

    def cut(ref, k):
        return ref[:, k * lanes : (k + 1) * lanes]

    blocks = half // lanes

    def scores(i, j):
        return lax.dot_general(
            sh[i], j, (((1,), (1,)), ((), ())), preferred_element_type=F32
        )

    def tile(ri, i, j, halves):
        s = scores(i, sh[pl.ds(j, halves)].reshape(halves * half, width))
        cols = [(j + a, slice(k * lanes, (k + 1) * lanes)) for a in range(halves) for k in range(blocks)]
        cm = [colmax[n, :, at] for n, at in cols]
        cs = [colsum[n, :, at] for n, at in cols]
        tag = [ct[n, 0:1, at] for n, at in cols]
        for r in range(blocks):
            at = slice(r * lanes, (r + 1) * lanes)
            rt, rm, rs = rowtag[ri, at, :], rowmax[ri, at, :], rowsum[ri, at, :]
            for k in range(len(cols)):
                v = jnp.where(rt == tag[k], s[at, k * lanes : (k + 1) * lanes], MASKED)
                e = jnp.exp(20.0 * v)
                rm, rs = jnp.maximum(rm, v), rs + e
                cm[k] = jnp.maximum(cm[k], jnp.max(v.reshape(lanes // 8, 8, lanes), axis=0))
                cs[k] = cs[k] + jnp.sum(e.reshape(lanes // 8, 8, lanes), axis=0)
            rowmax[ri, at, :], rowsum[ri, at, :] = rm, rs
        for k, (n, at) in enumerate(cols):
            colmax[n, :, at], colsum[n, :, at] = cm[k], cs[k]

    def own_tile(a):
        s = scores(a, sh[a])
        off = lax.broadcasted_iota(jnp.int32, (lanes, lanes), 0) != lax.broadcasted_iota(
            jnp.int32, (lanes, lanes), 1
        )
        for r in range(blocks):
            at = slice(r * lanes, (r + 1) * lanes)
            rt, rm, rs = rowtag[a, at, :], rowmax[a, at, :], rowsum[a, at, :]
            for k in range(blocks):
                hit = rt == ct[a, 0:1, k * lanes : (k + 1) * lanes]
                if r == k:
                    hit = hit & off
                v = jnp.where(hit, s[at, k * lanes : (k + 1) * lanes], MASKED)
                e = jnp.exp(20.0 * v)
                rm, rs = jnp.maximum(rm, v), rs + e
            rowmax[a, at, :], rowsum[a, at, :] = rm, rs

    group_of = 6

    def turn(t, carry):
        for first in range(0, count, group_of):

            @pl.when(t // group_of == first // group_of)
            def _(first=first):
                for k in range(first, min(first + group_of, count)):
                    for core in (0, 1):
                        what = events[core].get(k, [])
                        if what:

                            @pl.when((t == k) & (c == core))
                            def _(what=what):
                                for kind, q in what:
                                    event(kind, q)

        kind, ri, i, j = operands(t)

        @pl.when(kind == 0)
        def _():
            tile(ri, i, j, 1)

        @pl.when(kind == 1)
        def _():
            tile(ri, i, j, 2)

        @pl.when(kind == 2)
        def _():
            own_tile(ri)

        return carry

    lax.fori_loop(0, count, turn, 0)

    def flat(ref, ri, k, op):
        return op(
            jnp.transpose(ref[ri, k * lanes : (k + 1) * lanes, :]), axis=0, keepdims=True
        )

    places = {
        0: (x, z, c), 1: (x, zb, c), 2: (x, z2, c), 3: (xn, z3, c), 4: (x, z, 1 - c), 5: (x, zf, 1 - c),
    }

    def send_part(j, q):
        sy, sx = SENDS[q]
        xo, zo, co = places[j]
        return pltpu.make_async_remote_copy(
            part.at[SLOTS * q + j], back.at[SLOTS * q + j], b_s, b_r,
            device_id=dev(3 - xo if sx else xo, (y - sy + 4) % 4, zo, co), device_id_type=MESH,
        )

    for j in (4, 1, 2, 5, 3, 0):
        for a in (0, 1):
            top = jnp.max(colmax[2 * j + a], axis=0, keepdims=True)
            total = jnp.sum(colsum[2 * j + a], axis=0, keepdims=True)
            if j in ROWSLOT:
                ri = 2 * ROWSLOT[j] + a
                top = jnp.maximum(
                    top, jnp.concatenate([flat(rowmax, ri, k, jnp.max) for k in range(blocks)], axis=1)
                )
                total = total + jnp.concatenate(
                    [flat(rowsum, ri, k, jnp.sum) for k in range(blocks)], axis=1
                )
            for k in range(4):
                q = 4 * a + k
                at = SLOTS * q + j
                part[at, 0:1, 0:cap] = top[:, k * cap : (k + 1) * cap]
                part[at, 1:2, 0:cap] = total[:, k * cap : (k + 1) * cap]
                if at:
                    send_part(j, q).start()
    rest = pl.ds(1, SLOTS * GROUPS - 1)
    landed(back.at[rest], b_r)

    target8, rank8 = ids[0], ids[1]
    outs = [jnp.zeros((8, lanes), F32), jnp.zeros((8, lanes), F32)]
    for n in range(GROUPS):
        have = [(back if SLOTS * n + j else part)[SLOTS * n + j] for j in range(SLOTS)]
        top = functools.reduce(jnp.maximum, have)[0:1]
        mass = jnp.log(1.0 + functools.reduce(jnp.add, have)[1:2])
        for k, line in enumerate((top, mass)):
            found = jnp.take_along_axis(jnp.broadcast_to(line, (8, lanes)), rank8, axis=1)
            outs[k] = jnp.where(target8 == n, found, outs[k])
    for k in (0, 1):
        out_ref[k * rows // lanes : (k + 1) * rows // lanes] = outs[k][0 : rows // lanes]

    for n in range(1, GROUPS):
        send_tag(n).wait_send()
        for core in (0, 1):
            if ("W", n) not in sum(events[core].values(), []):
                pl.when(c == core)(send_rows(n).wait_send)
    for j in range(1, SLOTS):
        send_ct(j).wait_send()
    landed(part.at[rest], b_s)
    for q in range(GROUPS):
        forward(0, 1, q, ahead).wait_send()
        forward(0, 4, q, sibling).wait_send()
        forward(1, 2, q, ahead).wait_send()
        forward(1, 5, q, sibling).wait_send()
        forward(0, 3, q, across).wait_send()


def part_in_two(both_ref, best_ref, mass_ref):
    count = best_ref.shape[0]
    best_ref[...] = both_ref[0:count]
    mass_ref[...] = both_ref[count : 2 * count]


def body(embeddings, cluster_id, cluster_group):
    rows, width = embeddings.shape
    cap = rows * 3 // (2 * GROUPS)
    half, lanes = 4 * cap, 128
    dma = pltpu.SemaphoreType.DMA
    both = pl.pallas_call(
        functools.partial(kernel, cap),
        out_shape=jax.ShapeDtypeStruct((2 * rows // lanes, lanes), F32),
        in_specs=[
            pl.BlockSpec(memory_space=pltpu.VMEM),
            pl.BlockSpec(memory_space=pltpu.SMEM),
            pl.BlockSpec(memory_space=pl.ANY),
        ],
        out_specs=pl.BlockSpec(memory_space=pltpu.VMEM),
        scratch_shapes=[
            pltpu.VMEM((rows, width), F32),
            pltpu.VMEM((rows, width), BF16),
            pltpu.VMEM((GROUPS * cap, rows), BF16),
            pltpu.VMEM((GROUPS * cap, width), BF16),
            pltpu.VMEM((2 * SLOTS, half, width), BF16),
            pltpu.VMEM((GROUPS, 8, lanes), F32),
            pltpu.VMEM((GROUPS, 8, lanes), F32),
            pltpu.VMEM((2 * SLOTS, 8, half), F32),
            pltpu.VMEM((6, half, lanes), F32),
            pltpu.VMEM((6, half, lanes), F32),
            pltpu.VMEM((6, half, lanes), F32),
            pltpu.VMEM((2 * SLOTS, 8, half), F32),
            pltpu.VMEM((2 * SLOTS, 8, half), F32),
            pltpu.VMEM((SLOTS * GROUPS, 8, lanes), F32),
            pltpu.VMEM((SLOTS * GROUPS, 8, lanes), F32),
            pltpu.VMEM((2, 8, lanes), jnp.int32),
            dma((4,)),
            dma((GROUPS,)), dma((GROUPS,)),
            dma((SLOTS - 1, GROUPS)), dma((SLOTS - 1, GROUPS)),
            dma((GROUPS,)), dma((GROUPS,)),
            dma((SLOTS - 1,)), dma((SLOTS - 1,)),
            dma, dma,
        ],
        compiler_params=pltpu.CompilerParams(
            collective_id=0, has_side_effects=True, vmem_limit_bytes=60 * 2**20
        ),
    )(cluster_id.reshape(1, rows), cluster_group, embeddings)
    one = jax.ShapeDtypeStruct((rows // lanes, lanes), F32)
    best, mass = pl.pallas_call(part_in_two, out_shape=(one, one))(both)
    return best.reshape(rows), mass.reshape(rows)


def solution(mesh):
    in_specs = (P(("grp", "blk"), None), P(("grp", "blk")), P())
    out_specs = (P(("grp", "blk")), P(("grp", "blk")))
    return jax.shard_map(body, mesh=mesh, in_specs=in_specs, out_specs=out_specs, check_vma=False)
```

```python
import functools

import jax
import jax.numpy as jnp
from jax import lax
from jax.experimental import pallas as pl
from jax.experimental.pallas import tpu as pltpu
from jax.sharding import PartitionSpec as P

MESH = pl.DeviceIdType.MESH
F32 = jnp.float32
BF16 = jnp.bfloat16
GROUPS = 8
SLOTS = 6
MASKED = -30.0
SENDS = ((0, 0), (0, 1), (1, 0), (3, 0), (1, 1), (3, 1), (2, 0), (2, 1))

KINDS = {"n": 0, "w": 1, "s": 2, "p": 3}
SLOT_OF = {"E": 0, "F": 1, "G": 2, "K": 3, "D": 4, "H": 5}
PROGRAMS = (
    (
        "S1", "S2", "S3", "E0", "F0", "W1", "W2", "W3", "S4", "S5", "E1", "T0", "E2", "E3", "R0",
        ("s", 0, 0, 0, 0), "W4", "W5", "S6", "S7", "F1", "F2", "F3", "E4", "E5", "E6", "E7", ("s", 0, 1, 0, 1),
        ("n", 0, 0, 0, 1), "C3", "C4", "D0", "D1", "D2", "D3", "D4", "D5", "D6", "D7", "K0", "K1", "K2", "K3",
        "R3", ("w", 3, 0, 4, 0), ("w", 0, 0, 4, 0), "F4", "F5", ("n", 3, 0, 0, 1), "F6", "F7", "C1",
        ("w", 0, 0, 1, 0), ("w", 0, 1, 1, 0), ("w", 3, 0, 1, 0), "K4", "K5", "K6", "K7", ("w", 3, 1, 1, 0),
        "C5", "H0", "H1", "H2", "H3", "H4", "H5", "H6", "H7", ("w", 3, 0, 5, 0), ("w", 3, 1, 5, 0),
        ("w", 3, 1, 4, 0), "C2", "G0", "G1", "G2", "G3", "G4", "G5", "G6", "G7", "R2", ("w", 0, "z", 2, 0),
        ("w", 0, 0, 5, 0), "P0", ("w", 2, 0, 5, 0), "P2", "R1", ("w", 1, 0, 5, 0), "P1", ("n", 3, "x", 0, "x"),
        ("n", 3, 0, 2, 1), ("n", 3, "x", 2, "x"), ("p", 0, 0, 0, 0),
    ),
    (
        "S1", "S2", "S3", "E0", "F0", "W1", "W2", "W3", "S4", "S5", "E1", "T0", "E2", "E3", "R0",
        ("s", 0, 0, 0, 0), "G0", "W4", "W5", "S6", "S7", "F1", "F2", "F3", "E4", "E5", "E6", "E7",
        ("s", 0, 1, 0, 1), ("n", 0, 0, 0, 1), "G1", "C4", "D4", "D5", "D6", "D7", "R4", ("w", 4, 1, 0, 0),
        "P4", "G2", "G3", "F4", "F5", "F6", "F7", "C1", ("w", 0, 0, 1, 0), ("w", 0, 1, 1, 0), "C5", "H4", "H5",
        "H6", "H7", "R5", ("w", 5, 1, 0, 0), "G4", "G5", ("w", 5, 1, 1, 0), "C3", "K0", "K1", "K2", "K3", "R3",
        ("w", 3, 0, 1, 0), "H0", "H1", "H2", "H3", ("w", 3, 0, 5, 0), "G6", "G7", "D0", "D1", "D2", "D3",
        ("w", 3, 0, 4, 0), "C2", "R2", ("w", 0, "z", 2, 0), "P0", "P2", ("w", 5, 1, 2, 0), "P5",
        ("n", 3, 0, 0, 1), ("n", 3, 0, 2, 1), "K4", "K5", "K6", "K7", ("w", 3, 1, 1, 0), ("w", 3, 1, 5, 0),
        ("w", 3, 1, 4, 0), ("n", 3, "x", 0, "x"), ("n", 3, "x", 2, "x"), ("p", 0, 0, 0, 0),
    ),
)


def kernel(
    cap, cid_ref, cg_ref, emb_ref, out_ref,
    emb, unit, hot, outgo, sh, tagout, tagin, ct, rowtag,
    rowmax, rowsum, colmax, colsum, rowflat, part, back, ids,
    in_sem, a_s, a_r, f_s, f_r, t_s, t_r, ct_s, ct_r, b_s, b_r,
):
    rows, width = emb.shape
    half = 4 * cap
    lanes = 128
    g, b = lax.axis_index("grp"), lax.axis_index("blk")
    y, c = g // 2, g % 2
    x, z = b // 4, b % 4
    h, xb = x // 2, x % 2
    xn = 2 * h + 1 - xb
    step = 2 * c - 1
    zf = (z + step + 4) % 4
    zb = (z - step + 4) % 4
    z2 = (z + 2) % 4
    x3 = 3 - x

    def dev(px, py, pz, pc):
        return {"grp": 2 * py + pc, "blk": 4 * px + pz}

    z3 = z + 2 * c - 4 * ((z + 2 * c) // 4)
    holder = {
        1: dev(x, y, zf, c), 2: dev(x, y, z2, c), 3: dev(xn, y, z3, c),
        4: dev(x, y, z, 1 - c), 5: dev(x, y, zf, 1 - c),
    }
    owner = dict(holder)
    owner[1] = dev(x, y, zb, c)

    barrier = pltpu.get_barrier_semaphore()
    friends = []
    for dy in range(4):
        if dy:
            friends.append(dev(x, (y + dy) % 4, z, c))
        friends.append(dev(x3, (y + dy) % 4, z, c))
    friends += [
        dev(x, y, z, 1 - c), dev(x, y, zf, c), dev(x, y, zb, c), dev(x, y, z2, c),
        dev(xn, y, z, c), dev(xn, y, z2, c), dev(x, y, zf, 1 - c),
    ]
    for d in friends:
        pl.semaphore_signal(barrier, inc=1, device_id=d, device_id_type=MESH)

    parts = 4
    size = rows // parts

    def load(k):
        return pltpu.make_async_copy(
            emb_ref.at[pl.ds(k * size, size)], emb.at[pl.ds(k * size, size)], in_sem.at[k]
        )

    for k in range(parts):
        load(k).start()

    events, tiles = [], []
    for plan in PROGRAMS:
        when, work = {}, []
        for item in plan:
            if isinstance(item, str):
                when.setdefault(len(work), []).append((item[0], int(item[1])))
            else:
                work.append(item)
        events.append(when)
        tiles.append(work)
    count = len(tiles[0])
    zbit = z // 2

    def number(item):
        kind, i, a, j, b = item
        base = 256 * KINDS[kind] + 16 * (2 * j) + 2 * i
        if a == "z":
            return base, zbit, 2 * j + 1 - 2 * i + 16 * (2 * i - 2 * j)
        if a == "x":
            return base, xb, 17
        return base + a + 16 * b, 0, 0

    words = []
    for k in range(0, count, 3):
        both = []
        for work in tiles:
            word = 0
            for r, item in enumerate(work[k : k + 3]):
                base, bit, more = number(item)
                word = word + base * 1024**r + bit * (more * 1024**r)
            both.append(word)
        words.append(jnp.where(c == 0, both[0], both[1]))

    def operands(t):
        u, r = t // 3, t % 3
        word = words[0]
        for k in range(1, len(words)):
            word = jnp.where(u == k, words[k], word)
        code = jnp.where(r == 0, word, jnp.where(r == 1, word // 1024, word // 1024**2)) % 1024
        kind, j, i = code // 256, code // 16 % 16, code % 16
        return kind, i, j

    cid = cid_ref[...]
    group = jnp.zeros(cid.shape, jnp.int32)
    for k in range(cg_ref.shape[0]):
        group = jnp.where(cid == k, cg_ref[k], group)
    dy = ((group >> 1) - y) & 3
    other = (group & 1) ^ h
    target = jnp.zeros(cid.shape, jnp.int32)
    for n, (sy, sx) in enumerate(SENDS):
        target = jnp.where((dy == sy) & (other == sx), n, target)
    picks = jnp.where(
        lax.broadcasted_iota(jnp.int32, (GROUPS, rows), 0) == target, 1.0, 0.0
    ).astype(F32)
    earlier = jnp.where(
        lax.broadcasted_iota(jnp.int32, (rows, rows), 0)
        < lax.broadcasted_iota(jnp.int32, (rows, rows), 1),
        1.0,
        0.0,
    ).astype(BF16)
    before = jnp.dot(picks.astype(BF16), earlier, preferred_element_type=F32)
    rank = jnp.sum(picks * before, axis=0, keepdims=True).astype(jnp.int32)
    place = target * cap + rank
    hot[...] = jnp.where(
        lax.broadcasted_iota(jnp.int32, (GROUPS * cap, rows), 0) == place, 1.0, 0.0
    ).astype(BF16)
    ids[...] = jnp.zeros(ids.shape, jnp.int32)
    for k in range(rows // lanes):
        ids[0, k : k + 1, :] = target[:, k * lanes : (k + 1) * lanes]
        ids[1, k : k + 1, :] = rank[:, k * lanes : (k + 1) * lanes]

    names = jnp.broadcast_to((cid + 1).astype(F32), (8, rows)).astype(BF16)
    tags = lax.dot_general(
        names, hot[...], (((1,), (1,)), ((), ())), preferred_element_type=F32
    )
    tagout[...] = jnp.zeros(tagout.shape, F32)
    for k in range(GROUPS):
        tagout[k, :, 0:cap] = tags[:, k * cap : (k + 1) * cap]

    rowmax[...] = jnp.full(rowmax.shape, -1.0, F32)
    colmax[...] = jnp.full(colmax.shape, -1.0, F32)
    rowsum[...] = jnp.zeros(rowsum.shape, F32)
    colsum[...] = jnp.zeros(colsum.shape, F32)
    rowflat[:, 0:1, :] = jnp.full((2 * SLOTS, 1, half), -1.0, F32)
    rowflat[:, 1:2, :] = jnp.zeros((2 * SLOTS, 1, half), F32)
    part[...] = jnp.zeros(part.shape, F32)

    for k in range(parts):
        load(k).wait()
        v = emb[pl.ds(k * size, size)]
        scale = lax.rsqrt(jnp.sum(v * v, axis=1, keepdims=True) + 1e-06)
        unit[pl.ds(k * size, size)] = (v * scale).astype(BF16)
    packed = jnp.dot(hot[...], unit[...], preferred_element_type=F32).astype(BF16)
    sh[0, 0:cap] = packed[0:cap]
    outgo[...] = packed

    pl.semaphore_wait(barrier, len(friends))

    def chunk(slot, q):
        return sh.at[2 * slot + q // 4, pl.ds((q % 4) * cap, cap)]

    def dest(n):
        sy, sx = SENDS[n]
        return dev(x3 if sx else x, (y + sy) % 4, z, c)

    def send_tag(n):
        return pltpu.make_async_remote_copy(
            tagout.at[n], tagin.at[n], t_s.at[n], t_r.at[n], device_id=dest(n), device_id_type=MESH
        )

    def send_rows(n):
        return pltpu.make_async_remote_copy(
            outgo.at[pl.ds(n * cap, cap)], chunk(0, n), a_s.at[n], a_r.at[n],
            device_id=dest(n), device_id_type=MESH,
        )

    for n in range(1, GROUPS):
        send_tag(n).start()

    def landed(ref, sem):
        pltpu.make_async_copy(ref, ref, sem).wait()

    def send_ct(j):
        return pltpu.make_async_remote_copy(
            ct.at[pl.ds(0, 2)], ct.at[pl.ds(2 * j, 2)], ct_s.at[j - 1], ct_r.at[j - 1],
            device_id=holder[j], device_id_type=MESH,
        )

    def own_tags():
        for q in range(GROUPS):
            if q:
                landed(tagin.at[q], t_r.at[q])
            tag = tagin if q else tagout
            ct[q // 4, :, (q % 4) * cap : (q % 4 + 1) * cap] = tag[q, :, 0:cap]
        for j in range(1, SLOTS):
            send_ct(j).start()

    def row_tags(slot):
        for a in (0, 1):
            for k in range(half // lanes):
                v = ct[2 * slot + a, 0:1, k * lanes : (k + 1) * lanes]
                v = jnp.where(v == 0.0, -1.0, v)
                rowtag[2 * slot + a, pl.ds(k * lanes, lanes), :] = jnp.transpose(
                    jnp.broadcast_to(v, (lanes, lanes))
                )

    def forward(src, slot, q, to):
        return pltpu.make_async_remote_copy(
            chunk(src, q), chunk(slot, q), f_s.at[slot - 1, q], f_r.at[slot - 1, q],
            device_id=to, device_id_type=MESH,
        )

    ahead, across, sibling = dev(x, y, zf, c), dev(xn, y, z, c), dev(x, y, z, 1 - c)

    def flatten(slot):
        for n in (2 * slot, 2 * slot + 1):
            for k in range(half // lanes):
                at = slice(k * lanes, (k + 1) * lanes)
                for row, ref, op in ((0, rowmax, jnp.max), (1, rowsum, jnp.sum)):
                    rowflat[n, row : row + 1, at] = op(
                        jnp.transpose(ref[n, at, :]), axis=0, keepdims=True
                    )

    def event(kind, q):
        if kind == "T":
            return own_tags()
        if kind == "R":
            return row_tags(q)
        if kind == "C":
            return landed(ct.at[pl.ds(2 * q, 2)], ct_r.at[q - 1])
        if kind == "P":
            return flatten(q)
        if kind == "S":
            return send_rows(q).start()
        if kind == "W":
            return send_rows(q).wait_send()
        slot = SLOT_OF[kind]
        sem = a_r.at[q] if slot == 0 else f_r.at[slot - 1, q]
        if slot or q:
            landed(chunk(slot, q), sem)
        if slot == 0:
            forward(0, 1, q, ahead).start()
            pl.when(c == 0)(forward(0, 3, q, across).start)
            forward(0, 4, q, sibling).start()
        if slot == 1:
            forward(1, 2, q, ahead).start()
            forward(1, 5, q, sibling).start()
        if slot == 2:
            pl.when(c == 1)(forward(2, 3, q, across).start)

    blocks = half // lanes

    def scores(i, j):
        return lax.dot_general(
            sh[i], j, (((1,), (1,)), ((), ())), preferred_element_type=F32
        )

    def tile(i, j, halves):
        s = scores(i, sh[pl.ds(j, halves)].reshape(halves * half, width))
        cols = [(j + a, slice(k * lanes, (k + 1) * lanes)) for a in range(halves) for k in range(blocks)]
        cm = [colmax[n, :, at] for n, at in cols]
        cs = [colsum[n, :, at] for n, at in cols]
        tag = [ct[n, 0:1, at] for n, at in cols]
        for r in range(blocks):
            at = slice(r * lanes, (r + 1) * lanes)
            rt, rm, rs = rowtag[i, at, :], rowmax[i, at, :], rowsum[i, at, :]
            for k in range(len(cols)):
                v = jnp.where(rt == tag[k], s[at, k * lanes : (k + 1) * lanes], MASKED)
                e = jnp.exp(20.0 * v)
                rm, rs = jnp.maximum(rm, v), rs + e
                cm[k] = jnp.maximum(cm[k], jnp.max(v.reshape(lanes // 8, 8, lanes), axis=0))
                cs[k] = cs[k] + jnp.sum(e.reshape(lanes // 8, 8, lanes), axis=0)
            rowmax[i, at, :], rowsum[i, at, :] = rm, rs
        for k, (n, at) in enumerate(cols):
            colmax[n, :, at], colsum[n, :, at] = cm[k], cs[k]

    def own_tile(a):
        s = scores(a, sh[a])
        off = lax.broadcasted_iota(jnp.int32, (lanes, lanes), 0) != lax.broadcasted_iota(
            jnp.int32, (lanes, lanes), 1
        )
        for r in range(blocks):
            at = slice(r * lanes, (r + 1) * lanes)
            rt, rm, rs = rowtag[a, at, :], rowmax[a, at, :], rowsum[a, at, :]
            for k in range(blocks):
                hit = rt == ct[a, 0:1, k * lanes : (k + 1) * lanes]
                if r == k:
                    hit = hit & off
                v = jnp.where(hit, s[at, k * lanes : (k + 1) * lanes], MASKED)
                e = jnp.exp(20.0 * v)
                rm, rs = jnp.maximum(rm, v), rs + e
            rowmax[a, at, :], rowsum[a, at, :] = rm, rs

    group_of = 6

    def turn(t, carry):
        for first in range(0, count, group_of):

            @pl.when(t // group_of == first // group_of)
            def _(first=first):
                for k in range(first, min(first + group_of, count)):
                    for core in (0, 1):
                        what = events[core].get(k, [])
                        if what:

                            @pl.when((t == k) & (c == core))
                            def _(what=what):
                                for kind, q in what:
                                    event(kind, q)

        kind, i, j = operands(t)

        @pl.when(kind == 0)
        def _():
            tile(i, j, 1)

        @pl.when(kind == 1)
        def _():
            tile(i, j, 2)

        @pl.when(kind == 2)
        def _():
            own_tile(i)

        return carry

    lax.fori_loop(0, count, turn, 0)

    places = {
        0: (x, z, c), 1: (x, zb, c), 2: (x, z2, c), 3: (xn, z3, c), 4: (x, z, 1 - c), 5: (x, zf, 1 - c),
    }

    def send_part(j, q):
        sy, sx = SENDS[q]
        xo, zo, co = places[j]
        return pltpu.make_async_remote_copy(
            part.at[SLOTS * q + j], back.at[SLOTS * q + j], b_s, b_r,
            device_id=dev(3 - xo if sx else xo, (y - sy + 4) % 4, zo, co), device_id_type=MESH,
        )

    flatten(3)
    for j in (3, 2, 5, 1, 0, 4):
        for a in (0, 1):
            top = jnp.max(colmax[2 * j + a], axis=0, keepdims=True)
            total = jnp.sum(colsum[2 * j + a], axis=0, keepdims=True)
            top = jnp.maximum(top, rowflat[2 * j + a, 0:1, :])
            total = total + rowflat[2 * j + a, 1:2, :]
            for k in range(4):
                q = 4 * a + k
                at = SLOTS * q + j
                part[at, 0:1, 0:cap] = top[:, k * cap : (k + 1) * cap]
                part[at, 1:2, 0:cap] = total[:, k * cap : (k + 1) * cap]
                if at:
                    send_part(j, q).start()
    rest = pl.ds(1, SLOTS * GROUPS - 1)
    landed(back.at[rest], b_r)

    target8, rank8 = ids[0], ids[1]
    outs = [jnp.zeros((8, lanes), F32), jnp.zeros((8, lanes), F32)]
    for n in range(GROUPS):
        have = [(back if SLOTS * n + j else part)[SLOTS * n + j] for j in range(SLOTS)]
        top = functools.reduce(jnp.maximum, have)[0:1]
        mass = jnp.log(1.0 + functools.reduce(jnp.add, have)[1:2])
        for k, line in enumerate((top, mass)):
            found = jnp.take_along_axis(jnp.broadcast_to(line, (8, lanes)), rank8, axis=1)
            outs[k] = jnp.where(target8 == n, found, outs[k])
    for k in (0, 1):
        out_ref[k * rows // lanes : (k + 1) * rows // lanes] = outs[k][0 : rows // lanes]

    for n in range(1, GROUPS):
        send_tag(n).wait_send()
        for core in (0, 1):
            if ("W", n) not in sum(events[core].values(), []):
                pl.when(c == core)(send_rows(n).wait_send)
    for j in range(1, SLOTS):
        send_ct(j).wait_send()
    landed(part.at[rest], b_s)
    for q in range(GROUPS):
        forward(0, 1, q, ahead).wait_send()
        forward(0, 4, q, sibling).wait_send()
        forward(1, 2, q, ahead).wait_send()
        forward(1, 5, q, sibling).wait_send()
        forward(0, 3, q, across).wait_send()


def part_in_two(both_ref, best_ref, mass_ref):
    count = best_ref.shape[0]
    best_ref[...] = both_ref[0:count]
    mass_ref[...] = both_ref[count : 2 * count]


def body(embeddings, cluster_id, cluster_group):
    rows, width = embeddings.shape
    cap = rows * 3 // (2 * GROUPS)
    half, lanes = 4 * cap, 128
    dma = pltpu.SemaphoreType.DMA
    both = pl.pallas_call(
        functools.partial(kernel, cap),
        out_shape=jax.ShapeDtypeStruct((2 * rows // lanes, lanes), F32),
        in_specs=[
            pl.BlockSpec(memory_space=pltpu.VMEM),
            pl.BlockSpec(memory_space=pltpu.SMEM),
            pl.BlockSpec(memory_space=pl.ANY),
        ],
        out_specs=pl.BlockSpec(memory_space=pltpu.VMEM),
        scratch_shapes=[
            pltpu.VMEM((rows, width), F32),
            pltpu.VMEM((rows, width), BF16),
            pltpu.VMEM((GROUPS * cap, rows), BF16),
            pltpu.VMEM((GROUPS * cap, width), BF16),
            pltpu.VMEM((2 * SLOTS, half, width), BF16),
            pltpu.VMEM((GROUPS, 8, lanes), F32),
            pltpu.VMEM((GROUPS, 8, lanes), F32),
            pltpu.VMEM((2 * SLOTS, 8, half), F32),
            pltpu.VMEM((2 * SLOTS, half, lanes), F32),
            pltpu.VMEM((2 * SLOTS, half, lanes), F32),
            pltpu.VMEM((2 * SLOTS, half, lanes), F32),
            pltpu.VMEM((2 * SLOTS, 8, half), F32),
            pltpu.VMEM((2 * SLOTS, 8, half), F32),
            pltpu.VMEM((2 * SLOTS, 2, half), F32),
            pltpu.VMEM((SLOTS * GROUPS, 2, lanes), F32),
            pltpu.VMEM((SLOTS * GROUPS, 2, lanes), F32),
            pltpu.VMEM((2, 8, lanes), jnp.int32),
            dma((4,)),
            dma((GROUPS,)), dma((GROUPS,)),
            dma((SLOTS - 1, GROUPS)), dma((SLOTS - 1, GROUPS)),
            dma((GROUPS,)), dma((GROUPS,)),
            dma((SLOTS - 1,)), dma((SLOTS - 1,)),
            dma, dma,
        ],
        compiler_params=pltpu.CompilerParams(
            collective_id=0, has_side_effects=True, vmem_limit_bytes=60 * 2**20
        ),
    )(cluster_id.reshape(1, rows), cluster_group, embeddings)
    one = jax.ShapeDtypeStruct((rows // lanes, lanes), F32)
    best, mass = pl.pallas_call(part_in_two, out_shape=(one, one))(both)
    return best.reshape(rows), mass.reshape(rows)


def solution(mesh):
    in_specs = (P(("grp", "blk"), None), P(("grp", "blk")), P())
    out_specs = (P(("grp", "blk")), P(("grp", "blk")))
    return jax.shard_map(body, mesh=mesh, in_specs=in_specs, out_specs=out_specs, check_vma=False)
```

```python
import functools

import jax
import jax.numpy as jnp
from jax import lax
from jax.experimental import pallas as pl
from jax.experimental.pallas import tpu as pltpu
from jax.sharding import PartitionSpec as P

MESH = pl.DeviceIdType.MESH
F32 = jnp.float32
BF16 = jnp.bfloat16
GROUPS = 8
SLOTS = 6
MASKED = -30.0
SENDS = ((0, 0), (0, 1), (1, 0), (3, 0), (1, 1), (3, 1), (2, 0), (2, 1))

KINDS = {"n": 0, "w": 1, "s": 2, "p": 3}
SLOT_OF = {"E": 0, "F": 1, "G": 2, "K": 3, "D": 4, "H": 5}
PROGRAMS = (
    (
        "S1", "S2", "S3", "E0", "F0", "W1", "W2", "W3", "S4", "S5", "E1", "T0", "E2", "E3",
        "W4", "W5", "S6", "S7", "F1", "R0", ("s", 0, 0, 0, 0), "F2", "F3", "E4", "E5", "E6", "E7", ("s", 0, 1, 0, 1),
        ("n", 0, 0, 0, 1), "C3", "C4", "D0", "D1", "D2", "D3", "D4", "D5", "D6", "D7", "K0", "K1", "K2", "K3",
        "R3", ("w", 3, 0, 4, 0), ("w", 0, 0, 4, 0), "F4", "F5", ("n", 3, 0, 0, 1), "F6", "F7", "C1",
        ("w", 0, 0, 1, 0), ("w", 0, 1, 1, 0), ("w", 3, 0, 1, 0), "K4", "K5", "K6", "K7", ("w", 3, 1, 1, 0),
        "C5", "H0", "H1", "H2", "H3", "H4", "H5", "H6", "H7", ("w", 3, 0, 5, 0), ("w", 3, 1, 5, 0),
        ("w", 3, 1, 4, 0), "C2", "G0", "G1", "G2", "G3", "G4", "G5", "G6", "G7", "R2", ("w", 0, "z", 2, 0),
        ("w", 0, 0, 5, 0), "P0", ("w", 2, 0, 5, 0), "P2", "R1", ("w", 1, 0, 5, 0), "P1", ("n", 3, "x", 0, "x"),
        ("n", 3, 0, 2, 1), ("n", 3, "x", 2, "x"), ("p", 0, 0, 0, 0),
    ),
    (
        "S1", "S2", "S3", "E0", "F0", "W1", "W2", "W3", "S4", "S5", "E1", "T0", "E2", "E3",
        "G0", "W4", "W5", "S6", "S7", "F1", "R0", ("s", 0, 0, 0, 0), "F2", "F3", "E4", "E5", "E6", "E7",
        ("s", 0, 1, 0, 1), ("n", 0, 0, 0, 1), "G1", "C4", "D4", "D5", "D6", "D7", "R4", ("w", 4, 1, 0, 0),
        "P4", "G2", "G3", "F4", "F5", "F6", "F7", "C1", ("w", 0, 0, 1, 0), ("w", 0, 1, 1, 0), "C5", "H4", "H5",
        "H6", "H7", "R5", ("w", 5, 1, 0, 0), "G4", "G5", ("w", 5, 1, 1, 0), "C3", "K0", "K1", "K2", "K3", "R3",
        ("w", 3, 0, 1, 0), "H0", "H1", "H2", "H3", ("w", 3, 0, 5, 0), "G6", "G7", "D0", "D1", "D2", "D3",
        ("w", 3, 0, 4, 0), "C2", "R2", ("w", 0, "z", 2, 0), "P0", "P2", ("w", 5, 1, 2, 0), "P5",
        ("n", 3, 0, 0, 1), ("n", 3, 0, 2, 1), "K4", "K5", "K6", "K7", ("w", 3, 1, 1, 0), ("w", 3, 1, 5, 0),
        ("w", 3, 1, 4, 0), ("n", 3, "x", 0, "x"), ("n", 3, "x", 2, "x"), ("p", 0, 0, 0, 0),
    ),
)


def kernel(
    cap, cid_ref, cg_ref, emb_ref, out_ref,
    emb, unit, hot, outgo, sh, tagout, tagin, ct, rowtag,
    rowmax, rowsum, colmax, colsum, rowflat, part, back, ids,
    in_sem, a_s, a_r, f_s, f_r, t_s, t_r, ct_s, ct_r, b_s, b_r,
):
    rows, width = emb.shape
    half = 4 * cap
    lanes = 128
    g, b = lax.axis_index("grp"), lax.axis_index("blk")
    y, c = g // 2, g % 2
    x, z = b // 4, b % 4
    h, xb = x // 2, x % 2
    xn = 2 * h + 1 - xb
    step = 2 * c - 1
    zf = (z + step + 4) % 4
    zb = (z - step + 4) % 4
    z2 = (z + 2) % 4
    x3 = 3 - x

    def dev(px, py, pz, pc):
        return {"grp": 2 * py + pc, "blk": 4 * px + pz}

    z3 = z + 2 * c - 4 * ((z + 2 * c) // 4)
    holder = {
        1: dev(x, y, zf, c), 2: dev(x, y, z2, c), 3: dev(xn, y, z3, c),
        4: dev(x, y, z, 1 - c), 5: dev(x, y, zf, 1 - c),
    }
    owner = dict(holder)
    owner[1] = dev(x, y, zb, c)

    barrier = pltpu.get_barrier_semaphore()
    friends = []
    for dy in range(4):
        if dy:
            friends.append(dev(x, (y + dy) % 4, z, c))
        friends.append(dev(x3, (y + dy) % 4, z, c))
    friends += [
        dev(x, y, z, 1 - c), dev(x, y, zf, c), dev(x, y, zb, c), dev(x, y, z2, c),
        dev(xn, y, z, c), dev(xn, y, z2, c), dev(x, y, zf, 1 - c),
    ]
    for d in friends:
        pl.semaphore_signal(barrier, inc=1, device_id=d, device_id_type=MESH)

    parts = 4
    size = rows // parts

    def load(k):
        return pltpu.make_async_copy(
            emb_ref.at[pl.ds(k * size, size)], emb.at[pl.ds(k * size, size)], in_sem.at[k]
        )

    for k in range(parts):
        load(k).start()

    events, tiles = [], []
    for plan in PROGRAMS:
        when, work = {}, []
        for item in plan:
            if isinstance(item, str):
                when.setdefault(len(work), []).append((item[0], int(item[1])))
            else:
                work.append(item)
        events.append(when)
        tiles.append(work)
    count = len(tiles[0])
    zbit = z // 2

    def number(item):
        kind, i, a, j, b = item
        base = 256 * KINDS[kind] + 16 * (2 * j) + 2 * i
        if a == "z":
            return base, zbit, 2 * j + 1 - 2 * i + 16 * (2 * i - 2 * j)
        if a == "x":
            return base, xb, 17
        return base + a + 16 * b, 0, 0

    words = []
    for k in range(0, count, 3):
        both = []
        for work in tiles:
            word = 0
            for r, item in enumerate(work[k : k + 3]):
                base, bit, more = number(item)
                word = word + base * 1024**r + bit * (more * 1024**r)
            both.append(word)
        words.append(jnp.where(c == 0, both[0], both[1]))

    def operands(t):
        u, r = t // 3, t % 3
        word = words[0]
        for k in range(1, len(words)):
            word = jnp.where(u == k, words[k], word)
        code = jnp.where(r == 0, word, jnp.where(r == 1, word // 1024, word // 1024**2)) % 1024
        kind, j, i = code // 256, code // 16 % 16, code % 16
        return kind, i, j

    cid = cid_ref[...]
    group = jnp.zeros(cid.shape, jnp.int32)
    for k in range(cg_ref.shape[0]):
        group = jnp.where(cid == k, cg_ref[k], group)
    dy = ((group >> 1) - y) & 3
    other = (group & 1) ^ h
    target = jnp.zeros(cid.shape, jnp.int32)
    for n, (sy, sx) in enumerate(SENDS):
        target = jnp.where((dy == sy) & (other == sx), n, target)
    picks = jnp.where(
        lax.broadcasted_iota(jnp.int32, (GROUPS, rows), 0) == target, 1.0, 0.0
    ).astype(F32)
    earlier = jnp.where(
        lax.broadcasted_iota(jnp.int32, (rows, rows), 0)
        < lax.broadcasted_iota(jnp.int32, (rows, rows), 1),
        1.0,
        0.0,
    ).astype(BF16)
    before = jnp.dot(picks.astype(BF16), earlier, preferred_element_type=F32)
    rank = jnp.sum(picks * before, axis=0, keepdims=True).astype(jnp.int32)
    place = target * cap + rank
    hot[...] = jnp.where(
        lax.broadcasted_iota(jnp.int32, (GROUPS * cap, rows), 0) == place, 1.0, 0.0
    ).astype(BF16)
    ids[...] = jnp.zeros(ids.shape, jnp.int32)
    for k in range(rows // lanes):
        ids[0, k : k + 1, :] = target[:, k * lanes : (k + 1) * lanes]
        ids[1, k : k + 1, :] = rank[:, k * lanes : (k + 1) * lanes]

    names = jnp.broadcast_to((cid + 1).astype(F32), (8, rows)).astype(BF16)
    tags = lax.dot_general(
        names, hot[...], (((1,), (1,)), ((), ())), preferred_element_type=F32
    )
    tagout[...] = jnp.zeros(tagout.shape, F32)
    for k in range(GROUPS):
        tagout[k, :, 0:cap] = tags[:, k * cap : (k + 1) * cap]

    rowmax[...] = jnp.full(rowmax.shape, -1.0, F32)
    colmax[...] = jnp.full(colmax.shape, -1.0, F32)
    rowsum[...] = jnp.zeros(rowsum.shape, F32)
    colsum[...] = jnp.zeros(colsum.shape, F32)
    rowflat[:, 0:1, :] = jnp.full((2 * SLOTS, 1, half), -1.0, F32)
    rowflat[:, 1:2, :] = jnp.zeros((2 * SLOTS, 1, half), F32)
    part[...] = jnp.zeros(part.shape, F32)

    for k in range(parts):
        load(k).wait()
        v = emb[pl.ds(k * size, size)]
        scale = lax.rsqrt(jnp.sum(v * v, axis=1, keepdims=True) + 1e-06)
        unit[pl.ds(k * size, size)] = (v * scale).astype(BF16)
    packed = jnp.dot(hot[...], unit[...], preferred_element_type=F32).astype(BF16)
    sh[0, 0:cap] = packed[0:cap]
    outgo[...] = packed

    pl.semaphore_wait(barrier, len(friends))

    def chunk(slot, q):
        return sh.at[2 * slot + q // 4, pl.ds((q % 4) * cap, cap)]

    def dest(n):
        sy, sx = SENDS[n]
        return dev(x3 if sx else x, (y + sy) % 4, z, c)

    def send_tag(n):
        return pltpu.make_async_remote_copy(
            tagout.at[n], tagin.at[n], t_s.at[n], t_r.at[n], device_id=dest(n), device_id_type=MESH
        )

    def send_rows(n):
        return pltpu.make_async_remote_copy(
            outgo.at[pl.ds(n * cap, cap)], chunk(0, n), a_s.at[n], a_r.at[n],
            device_id=dest(n), device_id_type=MESH,
        )

    for n in range(1, GROUPS):
        send_tag(n).start()

    def landed(ref, sem):
        pltpu.make_async_copy(ref, ref, sem).wait()

    def send_ct(j):
        return pltpu.make_async_remote_copy(
            ct.at[pl.ds(0, 2)], ct.at[pl.ds(2 * j, 2)], ct_s.at[j - 1], ct_r.at[j - 1],
            device_id=holder[j], device_id_type=MESH,
        )

    def own_tags():
        for q in range(GROUPS):
            if q:
                landed(tagin.at[q], t_r.at[q])
            tag = tagin if q else tagout
            ct[q // 4, :, (q % 4) * cap : (q % 4 + 1) * cap] = tag[q, :, 0:cap]
        for j in range(1, SLOTS):
            send_ct(j).start()

    def row_tags(slot):
        for a in (0, 1):
            for k in range(half // lanes):
                v = ct[2 * slot + a, 0:1, k * lanes : (k + 1) * lanes]
                v = jnp.where(v == 0.0, -1.0, v)
                rowtag[2 * slot + a, pl.ds(k * lanes, lanes), :] = jnp.transpose(
                    jnp.broadcast_to(v, (lanes, lanes))
                )

    def forward(src, slot, q, to):
        return pltpu.make_async_remote_copy(
            chunk(src, q), chunk(slot, q), f_s.at[slot - 1, q], f_r.at[slot - 1, q],
            device_id=to, device_id_type=MESH,
        )

    ahead, across, sibling = dev(x, y, zf, c), dev(xn, y, z, c), dev(x, y, z, 1 - c)

    def flatten(slot):
        for n in (2 * slot, 2 * slot + 1):
            for k in range(half // lanes):
                at = slice(k * lanes, (k + 1) * lanes)
                for row, ref, op in ((0, rowmax, jnp.max), (1, rowsum, jnp.sum)):
                    rowflat[n, row : row + 1, at] = op(
                        jnp.transpose(ref[n, at, :]), axis=0, keepdims=True
                    )

    def event(kind, q):
        if kind == "T":
            return own_tags()
        if kind == "R":
            return row_tags(q)
        if kind == "C":
            return landed(ct.at[pl.ds(2 * q, 2)], ct_r.at[q - 1])
        if kind == "P":
            return flatten(q)
        if kind == "S":
            return send_rows(q).start()
        if kind == "W":
            return send_rows(q).wait_send()
        slot = SLOT_OF[kind]
        sem = a_r.at[q] if slot == 0 else f_r.at[slot - 1, q]
        if slot or q:
            landed(chunk(slot, q), sem)
        if slot == 0:
            forward(0, 1, q, ahead).start()
            pl.when(c == 0)(forward(0, 3, q, across).start)
            forward(0, 4, q, sibling).start()
        if slot == 1:
            forward(1, 2, q, ahead).start()
            forward(1, 5, q, sibling).start()
        if slot == 2:
            pl.when(c == 1)(forward(2, 3, q, across).start)

    blocks = half // lanes

    def scores(i, j):
        return lax.dot_general(
            sh[i], j, (((1,), (1,)), ((), ())), preferred_element_type=F32
        )

    def tile(i, j, halves):
        s = scores(i, sh[pl.ds(j, halves)].reshape(halves * half, width))
        cols = [(j + a, slice(k * lanes, (k + 1) * lanes)) for a in range(halves) for k in range(blocks)]
        cm = [colmax[n, :, at] for n, at in cols]
        cs = [colsum[n, :, at] for n, at in cols]
        tag = [ct[n, 0:1, at] for n, at in cols]
        for r in range(blocks):
            at = slice(r * lanes, (r + 1) * lanes)
            rt, rm, rs = rowtag[i, at, :], rowmax[i, at, :], rowsum[i, at, :]
            for k in range(len(cols)):
                v = jnp.where(rt == tag[k], s[at, k * lanes : (k + 1) * lanes], MASKED)
                e = jnp.exp(20.0 * v)
                rm, rs = jnp.maximum(rm, v), rs + e
                cm[k] = jnp.maximum(cm[k], jnp.max(v.reshape(lanes // 8, 8, lanes), axis=0))
                cs[k] = cs[k] + jnp.sum(e.reshape(lanes // 8, 8, lanes), axis=0)
            rowmax[i, at, :], rowsum[i, at, :] = rm, rs
        for k, (n, at) in enumerate(cols):
            colmax[n, :, at], colsum[n, :, at] = cm[k], cs[k]

    def own_tile(a):
        s = scores(a, sh[a])
        off = lax.broadcasted_iota(jnp.int32, (lanes, lanes), 0) != lax.broadcasted_iota(
            jnp.int32, (lanes, lanes), 1
        )
        for r in range(blocks):
            at = slice(r * lanes, (r + 1) * lanes)
            rt, rm, rs = rowtag[a, at, :], rowmax[a, at, :], rowsum[a, at, :]
            for k in range(blocks):
                hit = rt == ct[a, 0:1, k * lanes : (k + 1) * lanes]
                if r == k:
                    hit = hit & off
                v = jnp.where(hit, s[at, k * lanes : (k + 1) * lanes], MASKED)
                e = jnp.exp(20.0 * v)
                rm, rs = jnp.maximum(rm, v), rs + e
            rowmax[a, at, :], rowsum[a, at, :] = rm, rs

    group_of = 6

    def turn(t, carry):
        for first in range(0, count, group_of):

            @pl.when(t // group_of == first // group_of)
            def _(first=first):
                for k in range(first, min(first + group_of, count)):
                    for core in (0, 1):
                        what = events[core].get(k, [])
                        if what:

                            @pl.when((t == k) & (c == core))
                            def _(what=what):
                                for kind, q in what:
                                    event(kind, q)

        kind, i, j = operands(t)

        @pl.when(kind == 0)
        def _():
            tile(i, j, 1)

        @pl.when(kind == 1)
        def _():
            tile(i, j, 2)

        @pl.when(kind == 2)
        def _():
            own_tile(i)

        return carry

    lax.fori_loop(0, count, turn, 0)

    places = {
        0: (x, z, c), 1: (x, zb, c), 2: (x, z2, c), 3: (xn, z3, c), 4: (x, z, 1 - c), 5: (x, zf, 1 - c),
    }

    def send_part(j, q):
        sy, sx = SENDS[q]
        xo, zo, co = places[j]
        return pltpu.make_async_remote_copy(
            part.at[SLOTS * q + j], back.at[SLOTS * q + j], b_s, b_r,
            device_id=dev(3 - xo if sx else xo, (y - sy + 4) % 4, zo, co), device_id_type=MESH,
        )

    flatten(3)
    for j in (3, 2, 5, 1, 0, 4):
        for a in (0, 1):
            top = jnp.max(colmax[2 * j + a], axis=0, keepdims=True)
            total = jnp.sum(colsum[2 * j + a], axis=0, keepdims=True)
            top = jnp.maximum(top, rowflat[2 * j + a, 0:1, :])
            total = total + rowflat[2 * j + a, 1:2, :]
            for k in range(4):
                q = 4 * a + k
                at = SLOTS * q + j
                part[at, 0:1, 0:cap] = top[:, k * cap : (k + 1) * cap]
                part[at, 1:2, 0:cap] = total[:, k * cap : (k + 1) * cap]
                if at:
                    send_part(j, q).start()
    rest = pl.ds(1, SLOTS * GROUPS - 1)
    for n in range(1, GROUPS):
        send_tag(n).wait_send()
        for core in (0, 1):
            if ("W", n) not in sum(events[core].values(), []):
                pl.when(c == core)(send_rows(n).wait_send)
    for j in range(1, SLOTS):
        send_ct(j).wait_send()
    for q in range(GROUPS):
        forward(0, 1, q, ahead).wait_send()
        forward(0, 4, q, sibling).wait_send()
        forward(1, 2, q, ahead).wait_send()
        forward(1, 5, q, sibling).wait_send()
        forward(0, 3, q, across).wait_send()
    landed(part.at[rest], b_s)
    landed(back.at[rest], b_r)

    target8, rank8 = ids[0], ids[1]
    outs = [jnp.zeros((8, lanes), F32), jnp.zeros((8, lanes), F32)]
    for n in range(GROUPS):
        have = [(back if SLOTS * n + j else part)[SLOTS * n + j] for j in range(SLOTS)]
        top = functools.reduce(jnp.maximum, have)[0:1]
        mass = jnp.log(1.0 + functools.reduce(jnp.add, have)[1:2])
        for k, line in enumerate((top, mass)):
            found = jnp.take_along_axis(jnp.broadcast_to(line, (8, lanes)), rank8, axis=1)
            outs[k] = jnp.where(target8 == n, found, outs[k])
    for k in (0, 1):
        out_ref[k * rows // lanes : (k + 1) * rows // lanes] = outs[k][0 : rows // lanes]


def part_in_two(both_ref, best_ref, mass_ref):
    count = best_ref.shape[0]
    best_ref[...] = both_ref[0:count]
    mass_ref[...] = both_ref[count : 2 * count]


def body(embeddings, cluster_id, cluster_group):
    rows, width = embeddings.shape
    cap = rows * 3 // (2 * GROUPS)
    half, lanes = 4 * cap, 128
    dma = pltpu.SemaphoreType.DMA
    both = pl.pallas_call(
        functools.partial(kernel, cap),
        out_shape=jax.ShapeDtypeStruct((2 * rows // lanes, lanes), F32),
        in_specs=[
            pl.BlockSpec(memory_space=pltpu.VMEM),
            pl.BlockSpec(memory_space=pltpu.SMEM),
            pl.BlockSpec(memory_space=pl.ANY),
        ],
        out_specs=pl.BlockSpec(memory_space=pltpu.VMEM),
        scratch_shapes=[
            pltpu.VMEM((rows, width), F32),
            pltpu.VMEM((rows, width), BF16),
            pltpu.VMEM((GROUPS * cap, rows), BF16),
            pltpu.VMEM((GROUPS * cap, width), BF16),
            pltpu.VMEM((2 * SLOTS, half, width), BF16),
            pltpu.VMEM((GROUPS, 8, lanes), F32),
            pltpu.VMEM((GROUPS, 8, lanes), F32),
            pltpu.VMEM((2 * SLOTS, 8, half), F32),
            pltpu.VMEM((2 * SLOTS, half, lanes), F32),
            pltpu.VMEM((2 * SLOTS, half, lanes), F32),
            pltpu.VMEM((2 * SLOTS, half, lanes), F32),
            pltpu.VMEM((2 * SLOTS, 8, half), F32),
            pltpu.VMEM((2 * SLOTS, 8, half), F32),
            pltpu.VMEM((2 * SLOTS, 2, half), F32),
            pltpu.VMEM((SLOTS * GROUPS, 2, lanes), F32),
            pltpu.VMEM((SLOTS * GROUPS, 2, lanes), F32),
            pltpu.VMEM((2, 8, lanes), jnp.int32),
            dma((4,)),
            dma((GROUPS,)), dma((GROUPS,)),
            dma((SLOTS - 1, GROUPS)), dma((SLOTS - 1, GROUPS)),
            dma((GROUPS,)), dma((GROUPS,)),
            dma((SLOTS - 1,)), dma((SLOTS - 1,)),
            dma, dma,
        ],
        compiler_params=pltpu.CompilerParams(
            collective_id=0, has_side_effects=True, vmem_limit_bytes=60 * 2**20
        ),
    )(cluster_id.reshape(1, rows), cluster_group, embeddings)
    one = jax.ShapeDtypeStruct((rows // lanes, lanes), F32)
    best, mass = pl.pallas_call(part_in_two, out_shape=(one, one))(both)
    return best.reshape(rows), mass.reshape(rows)


def solution(mesh):
    in_specs = (P(("grp", "blk"), None), P(("grp", "blk")), P())
    out_specs = (P(("grp", "blk")), P(("grp", "blk")))
    return jax.shard_map(body, mesh=mesh, in_specs=in_specs, out_specs=out_specs, check_vma=False)
```

```python
import functools

import jax
import jax.numpy as jnp
from jax import lax
from jax.experimental import pallas as pl
from jax.experimental.pallas import tpu as pltpu
from jax.sharding import PartitionSpec as P

MESH = pl.DeviceIdType.MESH
F32 = jnp.float32
BF16 = jnp.bfloat16
GROUPS = 8
SLOTS = 6
MASKED = -30.0
SENDS = ((0, 0), (0, 1), (1, 0), (3, 0), (1, 1), (3, 1), (2, 0), (2, 1))

KINDS = {"n": 0, "w": 1, "s": 2, "p": 3}
SLOT_OF = {"E": 0, "F": 1, "G": 2, "K": 3, "D": 4, "H": 5}
PROGRAMS = (
    (
        "S1", "S2", "S3", "E0", "F0", "W1", "W2", "W3", "S4", "S5", "E1", "T0", "E2", "E3", "R0",
        ("s", 0, 0, 0, 0), "W4", "W5", "S6", "S7", "F1", "F2", "F3", "E4", "E5", "E6", "E7", ("s", 0, 1, 0, 1),
        ("n", 0, 0, 0, 1), "C3", "C4", "D0", "D1", "D2", "D3", "D4", "D5", "D6", "D7", "K0", "K1", "K2", "K3",
        "R3", ("w", 3, 0, 4, 0), ("w", 0, 0, 4, 0), "F4", "F5", ("n", 3, 0, 0, 1), "F6", "F7", "C1",
        ("w", 0, 0, 1, 0), ("w", 0, 1, 1, 0), ("w", 3, 0, 1, 0), "K4", "K5", "K6", "K7", ("w", 3, 1, 1, 0),
        "C5", "H0", "H1", "H2", "H3", "H4", "H5", "H6", "H7", ("w", 3, 0, 5, 0), ("w", 3, 1, 5, 0),
        ("w", 3, 1, 4, 0), "C2", "G0", "G1", "G2", "G3", "G4", "G5", "G6", "G7", "R2", ("w", 0, "z", 2, 0),
        ("w", 0, 0, 5, 0), "P0", ("w", 2, 0, 5, 0), "P2", "R1", ("w", 1, 0, 5, 0), "P1", ("n", 3, "x", 0, "x"),
        ("n", 3, 0, 2, 1), ("n", 3, "x", 2, "x"), ("p", 0, 0, 0, 0),
    ),
    (
        "S1", "S2", "S3", "E0", "F0", "W1", "W2", "W3", "S4", "S5", "E1", "T0", "E2", "E3", "R0",
        ("s", 0, 0, 0, 0), "G0", "W4", "W5", "S6", "S7", "F1", "F2", "F3", "E4", "E5", "E6", "E7",
        ("s", 0, 1, 0, 1), ("n", 0, 0, 0, 1), "G1", "C4", "D4", "D5", "D6", "D7", "R4", ("w", 4, 1, 0, 0),
        "P4", "G2", "G3", "F4", "F5", "F6", "F7", "C1", ("w", 0, 0, 1, 0), ("w", 0, 1, 1, 0), "C5", "H4", "H5",
        "H6", "H7", "R5", ("w", 5, 1, 0, 0), "G4", "G5", ("w", 5, 1, 1, 0), "C3", "K0", "K1", "K2", "K3", "R3",
        ("w", 3, 0, 1, 0), "H0", "H1", "H2", "H3", "G6", ("w", 3, 0, 5, 0), "G7", "D0", "D1", "D2", "D3",
        ("w", 3, 0, 4, 0), "C2", "R2", ("w", 0, "z", 2, 0), "P0", "P2", ("w", 5, 1, 2, 0), "P5",
        ("n", 3, 0, 0, 1), ("n", 3, 0, 2, 1), "K4", "K5", "K6", "K7", ("w", 3, 1, 1, 0), ("w", 3, 1, 5, 0),
        ("w", 3, 1, 4, 0), ("n", 3, "x", 0, "x"), ("n", 3, "x", 2, "x"), ("p", 0, 0, 0, 0),
    ),
)


def kernel(
    cap, cid_ref, cg_ref, emb_ref, out_ref,
    emb, unit, hot, outgo, sh, tagout, tagin, ct, rowtag,
    rowmax, rowsum, colmax, colsum, rowflat, part, back, ids,
    in_sem, a_s, a_r, f_s, f_r, t_s, t_r, ct_s, ct_r, b_s, b_r,
):
    rows, width = emb.shape
    half = 4 * cap
    lanes = 128
    g, b = lax.axis_index("grp"), lax.axis_index("blk")
    y, c = g // 2, g % 2
    x, z = b // 4, b % 4
    h, xb = x // 2, x % 2
    xn = 2 * h + 1 - xb
    step = 2 * c - 1
    zf = (z + step + 4) % 4
    zb = (z - step + 4) % 4
    z2 = (z + 2) % 4
    x3 = 3 - x

    def dev(px, py, pz, pc):
        return {"grp": 2 * py + pc, "blk": 4 * px + pz}

    z3 = z + 2 * c - 4 * ((z + 2 * c) // 4)
    holder = {
        1: dev(x, y, zf, c), 2: dev(x, y, z2, c), 3: dev(xn, y, z3, c),
        4: dev(x, y, z, 1 - c), 5: dev(x, y, zf, 1 - c),
    }
    owner = dict(holder)
    owner[1] = dev(x, y, zb, c)

    barrier = pltpu.get_barrier_semaphore()
    friends = []
    for dy in range(4):
        if dy:
            friends.append(dev(x, (y + dy) % 4, z, c))
        friends.append(dev(x3, (y + dy) % 4, z, c))
    friends += [
        dev(x, y, z, 1 - c), dev(x, y, zf, c), dev(x, y, zb, c), dev(x, y, z2, c),
        dev(xn, y, z, c), dev(xn, y, z2, c), dev(x, y, zf, 1 - c),
    ]
    for d in friends:
        pl.semaphore_signal(barrier, inc=1, device_id=d, device_id_type=MESH)

    parts = 4
    size = rows // parts

    def load(k):
        return pltpu.make_async_copy(
            emb_ref.at[pl.ds(k * size, size)], emb.at[pl.ds(k * size, size)], in_sem.at[k]
        )

    for k in range(parts):
        load(k).start()

    events, tiles = [], []
    for plan in PROGRAMS:
        when, work = {}, []
        for item in plan:
            if isinstance(item, str):
                when.setdefault(len(work), []).append((item[0], int(item[1])))
            else:
                work.append(item)
        events.append(when)
        tiles.append(work)
    count = len(tiles[0])
    zbit = z // 2

    def number(item):
        kind, i, a, j, b = item
        base = 256 * KINDS[kind] + 16 * (2 * j) + 2 * i
        if a == "z":
            return base, zbit, 2 * j + 1 - 2 * i + 16 * (2 * i - 2 * j)
        if a == "x":
            return base, xb, 17
        return base + a + 16 * b, 0, 0

    words = []
    for k in range(0, count, 3):
        both = []
        for work in tiles:
            word = 0
            for r, item in enumerate(work[k : k + 3]):
                base, bit, more = number(item)
                word = word + base * 1024**r + bit * (more * 1024**r)
            both.append(word)
        words.append(jnp.where(c == 0, both[0], both[1]))

    def operands(t):
        u, r = t // 3, t % 3
        word = words[0]
        for k in range(1, len(words)):
            word = jnp.where(u == k, words[k], word)
        code = jnp.where(r == 0, word, jnp.where(r == 1, word // 1024, word // 1024**2)) % 1024
        kind, j, i = code // 256, code // 16 % 16, code % 16
        return kind, i, j

    cid = cid_ref[...]
    group = jnp.zeros(cid.shape, jnp.int32)
    for k in range(cg_ref.shape[0]):
        group = jnp.where(cid == k, cg_ref[k], group)
    dy = ((group >> 1) - y) & 3
    other = (group & 1) ^ h
    target = jnp.zeros(cid.shape, jnp.int32)
    for n, (sy, sx) in enumerate(SENDS):
        target = jnp.where((dy == sy) & (other == sx), n, target)
    picks = jnp.where(
        lax.broadcasted_iota(jnp.int32, (GROUPS, rows), 0) == target, 1.0, 0.0
    ).astype(F32)
    earlier = jnp.where(
        lax.broadcasted_iota(jnp.int32, (rows, rows), 0)
        < lax.broadcasted_iota(jnp.int32, (rows, rows), 1),
        1.0,
        0.0,
    ).astype(BF16)
    before = jnp.dot(picks.astype(BF16), earlier, preferred_element_type=F32)
    rank = jnp.sum(picks * before, axis=0, keepdims=True).astype(jnp.int32)
    place = target * cap + rank
    hot[...] = jnp.where(
        lax.broadcasted_iota(jnp.int32, (GROUPS * cap, rows), 0) == place, 1.0, 0.0
    ).astype(BF16)
    ids[...] = jnp.zeros(ids.shape, jnp.int32)
    for k in range(rows // lanes):
        ids[0, k : k + 1, :] = target[:, k * lanes : (k + 1) * lanes]
        ids[1, k : k + 1, :] = rank[:, k * lanes : (k + 1) * lanes]

    names = jnp.broadcast_to((cid + 1).astype(F32), (8, rows)).astype(BF16)
    tags = lax.dot_general(
        names, hot[...], (((1,), (1,)), ((), ())), preferred_element_type=F32
    )
    tagout[...] = jnp.zeros(tagout.shape, F32)
    for k in range(GROUPS):
        tagout[k, :, 0:cap] = tags[:, k * cap : (k + 1) * cap]

    rowmax[...] = jnp.full(rowmax.shape, -1.0, F32)
    colmax[...] = jnp.full(colmax.shape, -1.0, F32)
    rowsum[...] = jnp.zeros(rowsum.shape, F32)
    colsum[...] = jnp.zeros(colsum.shape, F32)
    rowflat[:, 0:1, :] = jnp.full((2 * SLOTS, 1, half), -1.0, F32)
    rowflat[:, 1:2, :] = jnp.zeros((2 * SLOTS, 1, half), F32)
    part[...] = jnp.zeros(part.shape, F32)

    for k in range(parts):
        load(k).wait()
        v = emb[pl.ds(k * size, size)]
        scale = lax.rsqrt(jnp.sum(v * v, axis=1, keepdims=True) + 1e-06)
        unit[pl.ds(k * size, size)] = (v * scale).astype(BF16)
    packed = jnp.dot(hot[...], unit[...], preferred_element_type=F32).astype(BF16)
    sh[0, 0:cap] = packed[0:cap]
    outgo[...] = packed

    pl.semaphore_wait(barrier, len(friends))

    def chunk(slot, q):
        return sh.at[2 * slot + q // 4, pl.ds((q % 4) * cap, cap)]

    def dest(n):
        sy, sx = SENDS[n]
        return dev(x3 if sx else x, (y + sy) % 4, z, c)

    def send_tag(n):
        return pltpu.make_async_remote_copy(
            tagout.at[n], tagin.at[n], t_s.at[n], t_r.at[n], device_id=dest(n), device_id_type=MESH
        )

    def send_rows(n):
        return pltpu.make_async_remote_copy(
            outgo.at[pl.ds(n * cap, cap)], chunk(0, n), a_s.at[n], a_r.at[n],
            device_id=dest(n), device_id_type=MESH,
        )

    for n in range(1, GROUPS):
        send_tag(n).start()

    def landed(ref, sem):
        pltpu.make_async_copy(ref, ref, sem).wait()

    def send_ct(j):
        return pltpu.make_async_remote_copy(
            ct.at[pl.ds(0, 2)], ct.at[pl.ds(2 * j, 2)], ct_s.at[j - 1], ct_r.at[j - 1],
            device_id=holder[j], device_id_type=MESH,
        )

    def own_tags():
        for q in range(GROUPS):
            if q:
                landed(tagin.at[q], t_r.at[q])
            tag = tagin if q else tagout
            ct[q // 4, :, (q % 4) * cap : (q % 4 + 1) * cap] = tag[q, :, 0:cap]
        for j in range(1, SLOTS):
            send_ct(j).start()

    def row_tags(slot):
        for a in (0, 1):
            for k in range(half // lanes):
                v = ct[2 * slot + a, 0:1, k * lanes : (k + 1) * lanes]
                v = jnp.where(v == 0.0, -1.0, v)
                rowtag[2 * slot + a, pl.ds(k * lanes, lanes), :] = jnp.transpose(
                    jnp.broadcast_to(v, (lanes, lanes))
                )

    def forward(src, slot, q, to):
        return pltpu.make_async_remote_copy(
            chunk(src, q), chunk(slot, q), f_s.at[slot - 1, q], f_r.at[slot - 1, q],
            device_id=to, device_id_type=MESH,
        )

    ahead, across, sibling = dev(x, y, zf, c), dev(xn, y, z, c), dev(x, y, z, 1 - c)

    def flatten(slot):
        for n in (2 * slot, 2 * slot + 1):
            for k in range(half // lanes):
                at = slice(k * lanes, (k + 1) * lanes)
                for row, ref, op in ((0, rowmax, jnp.max), (1, rowsum, jnp.sum)):
                    rowflat[n, row : row + 1, at] = op(
                        jnp.transpose(ref[n, at, :]), axis=0, keepdims=True
                    )

    def event(kind, q):
        if kind == "T":
            return own_tags()
        if kind == "R":
            return row_tags(q)
        if kind == "C":
            return landed(ct.at[pl.ds(2 * q, 2)], ct_r.at[q - 1])
        if kind == "P":
            return flatten(q)
        if kind == "S":
            return send_rows(q).start()
        if kind == "W":
            return send_rows(q).wait_send()
        slot = SLOT_OF[kind]
        sem = a_r.at[q] if slot == 0 else f_r.at[slot - 1, q]
        if slot or q:
            landed(chunk(slot, q), sem)
        if slot == 0:
            forward(0, 1, q, ahead).start()
            pl.when(c == 0)(forward(0, 3, q, across).start)
            forward(0, 4, q, sibling).start()
        if slot == 1:
            forward(1, 2, q, ahead).start()
            forward(1, 5, q, sibling).start()
        if slot == 2:
            pl.when(c == 1)(forward(2, 3, q, across).start)

    blocks = half // lanes

    def scores(i, j):
        return lax.dot_general(
            sh[i], j, (((1,), (1,)), ((), ())), preferred_element_type=F32
        )

    def tile(i, j, halves):
        s = scores(i, sh[pl.ds(j, halves)].reshape(halves * half, width))
        cols = [(j + a, slice(k * lanes, (k + 1) * lanes)) for a in range(halves) for k in range(blocks)]
        cm = [colmax[n, :, at] for n, at in cols]
        cs = [colsum[n, :, at] for n, at in cols]
        tag = [ct[n, 0:1, at] for n, at in cols]
        for r in range(blocks):
            at = slice(r * lanes, (r + 1) * lanes)
            rt, rm, rs = rowtag[i, at, :], rowmax[i, at, :], rowsum[i, at, :]
            for k in range(len(cols)):
                v = jnp.where(rt == tag[k], s[at, k * lanes : (k + 1) * lanes], MASKED)
                e = jnp.exp(20.0 * v)
                rm, rs = jnp.maximum(rm, v), rs + e
                cm[k] = jnp.maximum(cm[k], jnp.max(v.reshape(lanes // 8, 8, lanes), axis=0))
                cs[k] = cs[k] + jnp.sum(e.reshape(lanes // 8, 8, lanes), axis=0)
            rowmax[i, at, :], rowsum[i, at, :] = rm, rs
        for k, (n, at) in enumerate(cols):
            colmax[n, :, at], colsum[n, :, at] = cm[k], cs[k]

    def own_tile(a):
        s = scores(a, sh[a])
        off = lax.broadcasted_iota(jnp.int32, (lanes, lanes), 0) != lax.broadcasted_iota(
            jnp.int32, (lanes, lanes), 1
        )
        for r in range(blocks):
            at = slice(r * lanes, (r + 1) * lanes)
            rt, rm, rs = rowtag[a, at, :], rowmax[a, at, :], rowsum[a, at, :]
            for k in range(blocks):
                hit = rt == ct[a, 0:1, k * lanes : (k + 1) * lanes]
                if r == k:
                    hit = hit & off
                v = jnp.where(hit, s[at, k * lanes : (k + 1) * lanes], MASKED)
                e = jnp.exp(20.0 * v)
                rm, rs = jnp.maximum(rm, v), rs + e
            rowmax[a, at, :], rowsum[a, at, :] = rm, rs

    group_of = 6

    def turn(t, carry):
        for first in range(0, count, group_of):

            @pl.when(t // group_of == first // group_of)
            def _(first=first):
                for k in range(first, min(first + group_of, count)):
                    for core in (0, 1):
                        what = events[core].get(k, [])
                        if what:

                            @pl.when((t == k) & (c == core))
                            def _(what=what):
                                for kind, q in what:
                                    event(kind, q)

        kind, i, j = operands(t)

        @pl.when(kind == 0)
        def _():
            tile(i, j, 1)

        @pl.when(kind == 1)
        def _():
            tile(i, j, 2)

        @pl.when(kind == 2)
        def _():
            own_tile(i)

        return carry

    lax.fori_loop(0, count, turn, 0)

    places = {
        0: (x, z, c), 1: (x, zb, c), 2: (x, z2, c), 3: (xn, z3, c), 4: (x, z, 1 - c), 5: (x, zf, 1 - c),
    }

    def send_part(j, q):
        sy, sx = SENDS[q]
        xo, zo, co = places[j]
        return pltpu.make_async_remote_copy(
            part.at[SLOTS * q + j], back.at[SLOTS * q + j], b_s, b_r,
            device_id=dev(3 - xo if sx else xo, (y - sy + 4) % 4, zo, co), device_id_type=MESH,
        )

    flatten(3)
    for j in (3, 2, 5, 1, 0, 4):
        for a in (0, 1):
            top = jnp.max(colmax[2 * j + a], axis=0, keepdims=True)
            total = jnp.sum(colsum[2 * j + a], axis=0, keepdims=True)
            top = jnp.maximum(top, rowflat[2 * j + a, 0:1, :])
            total = total + rowflat[2 * j + a, 1:2, :]
            for k in range(4):
                q = 4 * a + k
                at = SLOTS * q + j
                part[at, 0:1, 0:cap] = top[:, k * cap : (k + 1) * cap]
                part[at, 1:2, 0:cap] = total[:, k * cap : (k + 1) * cap]
                if at:
                    send_part(j, q).start()
    rest = pl.ds(1, SLOTS * GROUPS - 1)
    landed(back.at[rest], b_r)

    target8, rank8 = ids[0], ids[1]
    outs = [jnp.zeros((8, lanes), F32), jnp.zeros((8, lanes), F32)]
    for n in range(GROUPS):
        have = [(back if SLOTS * n + j else part)[SLOTS * n + j] for j in range(SLOTS)]
        top = functools.reduce(jnp.maximum, have)[0:1]
        mass = jnp.log(1.0 + functools.reduce(jnp.add, have)[1:2])
        for k, line in enumerate((top, mass)):
            found = jnp.take_along_axis(jnp.broadcast_to(line, (8, lanes)), rank8, axis=1)
            outs[k] = jnp.where(target8 == n, found, outs[k])
    for k in (0, 1):
        out_ref[k * rows // lanes : (k + 1) * rows // lanes] = outs[k][0 : rows // lanes]

    for n in range(1, GROUPS):
        send_tag(n).wait_send()
        for core in (0, 1):
            if ("W", n) not in sum(events[core].values(), []):
                pl.when(c == core)(send_rows(n).wait_send)
    for j in range(1, SLOTS):
        send_ct(j).wait_send()
    landed(part.at[rest], b_s)
    for q in range(GROUPS):
        forward(0, 1, q, ahead).wait_send()
        forward(0, 4, q, sibling).wait_send()
        forward(1, 2, q, ahead).wait_send()
        forward(1, 5, q, sibling).wait_send()
        forward(0, 3, q, across).wait_send()


def part_in_two(both_ref, best_ref, mass_ref):
    count = best_ref.shape[0]
    best_ref[...] = both_ref[0:count]
    mass_ref[...] = both_ref[count : 2 * count]


def body(embeddings, cluster_id, cluster_group):
    rows, width = embeddings.shape
    cap = rows * 3 // (2 * GROUPS)
    half, lanes = 4 * cap, 128
    dma = pltpu.SemaphoreType.DMA
    both = pl.pallas_call(
        functools.partial(kernel, cap),
        out_shape=jax.ShapeDtypeStruct((2 * rows // lanes, lanes), F32),
        in_specs=[
            pl.BlockSpec(memory_space=pltpu.VMEM),
            pl.BlockSpec(memory_space=pltpu.SMEM),
            pl.BlockSpec(memory_space=pl.ANY),
        ],
        out_specs=pl.BlockSpec(memory_space=pltpu.VMEM),
        scratch_shapes=[
            pltpu.VMEM((rows, width), F32),
            pltpu.VMEM((rows, width), BF16),
            pltpu.VMEM((GROUPS * cap, rows), BF16),
            pltpu.VMEM((GROUPS * cap, width), BF16),
            pltpu.VMEM((2 * SLOTS, half, width), BF16),
            pltpu.VMEM((GROUPS, 8, lanes), F32),
            pltpu.VMEM((GROUPS, 8, lanes), F32),
            pltpu.VMEM((2 * SLOTS, 8, half), F32),
            pltpu.VMEM((2 * SLOTS, half, lanes), F32),
            pltpu.VMEM((2 * SLOTS, half, lanes), F32),
            pltpu.VMEM((2 * SLOTS, half, lanes), F32),
            pltpu.VMEM((2 * SLOTS, 8, half), F32),
            pltpu.VMEM((2 * SLOTS, 8, half), F32),
            pltpu.VMEM((2 * SLOTS, 2, half), F32),
            pltpu.VMEM((SLOTS * GROUPS, 2, lanes), F32),
            pltpu.VMEM((SLOTS * GROUPS, 2, lanes), F32),
            pltpu.VMEM((2, 8, lanes), jnp.int32),
            dma((4,)),
            dma((GROUPS,)), dma((GROUPS,)),
            dma((SLOTS - 1, GROUPS)), dma((SLOTS - 1, GROUPS)),
            dma((GROUPS,)), dma((GROUPS,)),
            dma((SLOTS - 1,)), dma((SLOTS - 1,)),
            dma, dma,
        ],
        compiler_params=pltpu.CompilerParams(
            collective_id=0, has_side_effects=True, vmem_limit_bytes=60 * 2**20
        ),
    )(cluster_id.reshape(1, rows), cluster_group, embeddings)
    one = jax.ShapeDtypeStruct((rows // lanes, lanes), F32)
    best, mass = pl.pallas_call(part_in_two, out_shape=(one, one))(both)
    return best.reshape(rows), mass.reshape(rows)


def solution(mesh):
    in_specs = (P(("grp", "blk"), None), P(("grp", "blk")), P())
    out_specs = (P(("grp", "blk")), P(("grp", "blk")))
    return jax.shard_map(body, mesh=mesh, in_specs=in_specs, out_specs=out_specs, check_vma=False)
```
